32 devices in a mesh: rep: 16 (over z, x, core), shard: 2 (over y).
Axes of the slice: x: 2, y: 2, z: 4, core: 2. Of those that a mesh axis runs over, the one named last changes fastest.
Arguments:
- tokens: bfloat16 [32768, 768], P(('rep', 'shard')), may hold values from -6 to 6
- segments: int32 [32, 1024], P(('rep', 'shard')), may hold values from 0 to 3, never falling along the last dimension, each value on 1 to 512 neighbouring positions
- attn_gain: bfloat16 [768], P('shard'), may hold values from 0.099609375 to 1.8984375
- attn_shift: bfloat16 [768], P('shard'), may hold values from -1.5 to 1.5
- qkv_weight: bfloat16 [768, 2304], P('shard'), may hold values from -0.21875 to 0.21875
- qkv_bias: bfloat16 [2304], P('shard'), may hold values from -1.5 to 1.5
- proj_weight: bfloat16 [768, 768], P('shard'), may hold values from -1.75 to 1.75
- proj_bias: bfloat16 [768], P('shard'), may hold values from -1.5 to 1.5
- mlp_gain: bfloat16 [768], P('shard'), may hold values from 0.099609375 to 1.8984375
- mlp_shift: bfloat16 [768], P('shard'), may hold values from -1.5 to 1.5
- up_weight: bfloat16 [768, 3072], P('shard'), may hold values from -0.21875 to 0.21875
- up_bias: bfloat16 [3072], P('shard'), may hold values from -1.5 to 1.5
- down_weight: bfloat16 [3072, 768], P('shard'), may hold values from -0.109375 to 0.109375
- down_bias: bfloat16 [768], P('shard'), may hold values from -1.5 to 1.5
- cotangent: bfloat16 [32768, 768], P(('rep', 'shard')), may hold values from -6 to 6
Outputs:
- block_out: bfloat16 [32768, 768], P(('rep', 'shard'))
- tokens_grad: float32 [32768, 768], P(('rep', 'shard'))
- attn_gain_grad: float32 [768], P('shard')
- attn_shift_grad: float32 [768], P('shard')
- qkv_weight_grad: float32 [768, 2304], P('shard')
- qkv_bias_grad: float32 [2304], P('shard')
- proj_weight_grad: float32 [768, 768], P('shard')
- proj_bias_grad: float32 [768], P('shard')
- mlp_gain_grad: float32 [768], P('shard')
- mlp_shift_grad: float32 [768], P('shard')
- up_weight_grad: float32 [768, 3072], P('shard')
- up_bias_grad: float32 [3072], P('shard')
- down_weight_grad: float32 [3072, 768], P('shard')
- down_bias_grad: float32 [768], P('shard')
The draws below stay inside these ranges and needn't reach their ends.
Inputs may be any that keep to these rules, and one draw needn't show every extreme that they name: `segments`: documents are numbered from 0 in each sequence, in order along it; every number up to the largest occurs.
All inputs are finite; a program needn't handle non-finite values.
Results may differ from the reference program's by a relative error of at most 0.017.
Values may be sent and summed in bfloat16 or wider, within the bound.
No kernel may reach another device: no remote copies, remote signals or barrier semaphores. Data moves between devices by JAX's collectives and lax.ppermute only.
A program may use at most 192 MiB of HBM per device.

```python
import math
import jax
import jax.numpy as jnp
import numpy as np
from jax import lax

D = 768
FF = 3072
HEADS = 12
HEAD_DIM = 64
ROT = 16
LENGTH = 1024
SEQS = 32
TOKENS = 32768


def block_levels(own_key, dims, cuts, smallest, largest):
    def one(axis_at, parts):
        draws = jax.random.uniform(jax.random.fold_in(jax.random.fold_in(own_key, 6), axis_at), (parts,), jnp.float32, smallest / len(cuts), largest / len(cuts))
        return jnp.repeat(jnp.exp(draws), dims[axis_at] // parts).reshape((-1,) + (1,) * (len(dims) - axis_at - 1))

    loudness = one(*cuts[0])
    for cut in cuts[1:]:
        loudness = loudness * one(*cut)
    return loudness


def length_profile(amount, total, limit, lean):
    loads = [(1 << 20) // math.isqrt(standing ** lean) + 1 for standing in range(2, amount + 1)]
    surplus, holding = total - limit - (amount - 1), [1] * (amount - 1)
    while surplus > 0:
        candidates = [i for i in range(amount - 1) if holding[i] < limit]
        pool, budget = sum([loads[i] for i in candidates]), surplus
        for i in candidates:
            addition = min(limit - holding[i], max(1, budget * loads[i] // pool), surplus)
            holding[i] = holding[i] + addition
            surplus = surplus - addition
    return np.array([limit] + holding)


def ragged(key, amount, total, reach, slope):
    if amount == 2:
        one = jax.random.randint(key, (), max(1, total - reach), min(reach, total - 1) + 1)
        return jnp.stack([one, total - one])
    tallies = jnp.asarray(length_profile(amount, total, reach, slope), jnp.int32)
    twos = (amount - 1) // 2
    donor, sink = tallies[1:1 + 2 * twos:2], tallies[2:2 + 2 * twos:2]
    slack = jnp.minimum(donor - 1, reach - sink)
    passed = jax.random.randint(jax.random.fold_in(key, 1), (twos,), 0, 1 << 20) % (slack + 1)
    tallies = tallies.at[1:1 + 2 * twos:2].set(donor - passed).at[2:2 + 2 * twos:2].set(sink + passed)
    return tallies[jax.random.permutation(jax.random.fold_in(key, 2), amount)]


def scatter_about(rng, shape, scale, bound, shards=(), kind=jnp.bfloat16):
    level = block_levels(rng, shape, shards, -0.22, 0.18) if shards else 1.0
    result = jax.random.normal(rng, shape, jnp.float32) * scale * level
    return jnp.minimum(jnp.maximum(result, -bound), bound).astype(kind)


def setup_inputs(seed: int = 0) -> dict:
    streams_of = jax.random.split(jax.random.key(seed), 16)
    return {
        "tokens": scatter_about(streams_of[0], (TOKENS, D), 1.0, 6.0, ((0, 32),)),
        "segments": jax.vmap(lambda own: jnp.searchsorted(jnp.cumsum(ragged(own, max(3, LENGTH // 256), LENGTH, LENGTH // 2, 2)), jnp.arange(LENGTH), side="right"))(jax.random.split(streams_of[1], SEQS)).reshape((SEQS, LENGTH)).astype(jnp.int32),
        "attn_gain": jnp.clip(1.0 + 0.18 * jax.random.normal(streams_of[2], (D,), jnp.float32), 0.099609375, 1.8984375).astype(jnp.bfloat16),
        "attn_shift": scatter_about(streams_of[3], (D,), 0.3, 1.5, ((0, 2),)),
        "qkv_weight": scatter_about(streams_of[4], (D, 3 * D), D ** -0.5, 0.21875, ((0, 2),)),
        "qkv_bias": scatter_about(streams_of[5], (3 * D,), 0.3, 1.5, ((0, 2),)),
        "proj_weight": scatter_about(streams_of[6], (D, D), (max(1, D // 64)) ** -0.5, 1.75, ((0, 2),)),
        "proj_bias": scatter_about(streams_of[7], (D,), 0.3, 1.5, ((0, 2),)),
        "mlp_gain": jnp.clip(1.0 + 0.18 * jax.random.normal(streams_of[8], (D,), jnp.float32), 0.099609375, 1.8984375).astype(jnp.bfloat16),
        "mlp_shift": scatter_about(streams_of[9], (D,), 0.3, 1.5, ((0, 2),)),
        "up_weight": scatter_about(streams_of[10], (D, FF), D ** -0.5, 0.21875, ((0, 2),)),
        "up_bias": scatter_about(streams_of[11], (FF,), 0.3, 1.5, ((0, 2),)),
        "down_weight": scatter_about(streams_of[12], (FF, D), FF ** -0.5, 0.109375, ((0, 2),)),
        "down_bias": scatter_about(streams_of[13], (D,), 0.3, 1.5, ((0, 2),)),
        "cotangent": scatter_about(streams_of[14], (TOKENS, D), 1.0, 6.0, ((0, 32),)),
    }


EPS = 1e-05
HIGH = lax.Precision.HIGHEST

@jax.custom_vjp
def low(v):
    return lax.optimization_barrier(v.astype(jnp.bfloat16)).astype(jnp.float32)

@jax.custom_vjp
def low_back(v):
    return v

def low_keep(v):
    return (low(v), None)

def low_pass(kept, grad):
    return (grad,)

def back_keep(v):
    return (v, None)

def back_low(kept, grad):
    return (low(grad),)
low.defvjp(low_keep, low_pass)
low_back.defvjp(back_keep, back_low)

def layer_norm(values, gain, shift):
    center = values - lax.optimization_barrier(jnp.mean(values, axis=-1, keepdims=True))
    spread = lax.optimization_barrier(jnp.mean(center * center, axis=-1, keepdims=True))
    return center * lax.rsqrt(spread + EPS) * gain + shift

def gelu_exact(values):
    return 0.5 * values * (1.0 + lax.erf(values * (1.0 / math.sqrt(2.0))))

def rotary_tables(segments):
    row_count, length = segments.shape
    position = jnp.arange(length, dtype=jnp.int32)
    change = jnp.concatenate([jnp.ones((row_count, 1), dtype=bool), segments[:, 1:] != segments[:, :-1]], axis=1)
    doc_start = lax.cummax(jnp.where(change, position[None, :], 0).astype(jnp.int32), axis=1)
    doc_place = (position[None, :] - doc_start).astype(jnp.float32)
    half_rot = ROT // 2
    frequency = 10000.0 ** (-2.0 * jnp.arange(half_rot, dtype=jnp.float32) / ROT)
    angles = doc_place[..., None] * frequency
    cosine = jnp.concatenate([jnp.cos(angles), jnp.cos(angles)], axis=-1)
    sine = jnp.concatenate([jnp.sin(angles), jnp.sin(angles)], axis=-1)
    return (cosine, sine)

def rotate(values, cosine, sine):
    turned_part = values[..., :ROT]
    first_half = turned_part[..., :ROT // 2]
    second_half = turned_part[..., ROT // 2:]
    swapped = jnp.concatenate([-second_half, first_half], axis=-1)
    return jnp.concatenate([turned_part * cosine + swapped * sine, values[..., ROT:]], axis=-1)

def attend(members):
    queries, keys, values, segment = members
    length = segment.shape[-1]
    raw = jnp.einsum('gqhd,gkhd->ghqk', queries, keys, precision=HIGH)
    scores = low_back(raw * HEAD_DIM ** (-0.5))
    position = jnp.arange(length, dtype=jnp.int32)
    allowed = (segment[:, :, None] == segment[:, None, :]) & (position[:, None] >= position[None, :])[None]
    scores = jnp.where(allowed[:, None], scores, -1e+30)
    row_top = lax.optimization_barrier(jnp.max(scores, axis=-1, keepdims=True))
    weight = jnp.exp(scores - row_top)
    soft_probs = weight / lax.optimization_barrier(jnp.sum(weight, axis=-1, keepdims=True))
    return jnp.einsum('ghqk,gkhd->gqhd', low(soft_probs), values, precision=HIGH)

def block(tokens, attn_gain, attn_shift, qkv_weight, qkv_bias, proj_weight, proj_bias, mlp_gain, mlp_shift, up_weight, up_bias, down_weight, down_bias, cosine, sine, segments):
    normed_attn = low(layer_norm(tokens, attn_gain, attn_shift))
    mixed_proj = low_back(jnp.dot(normed_attn, qkv_weight, precision=HIGH) + qkv_bias)
    mixed_proj = mixed_proj.reshape(TOKENS, 3, HEADS, HEAD_DIM)
    queries = low(rotate(mixed_proj[:, 0], cosine, sine))
    keys = low(rotate(mixed_proj[:, 1], cosine, sine))
    values = low(mixed_proj[:, 2])
    group_size = math.gcd(SEQS, max(1, 4096 // LENGTH))
    group_shape = (SEQS // group_size, group_size, LENGTH, HEADS, HEAD_DIM)
    heads = lax.map(jax.checkpoint(attend), (queries.reshape(group_shape), keys.reshape(group_shape), values.reshape(group_shape), segments.reshape(SEQS // group_size, group_size, LENGTH)))
    heads = low_back(low(heads.reshape(TOKENS, D)))
    branch_attn = jnp.dot(heads, proj_weight, precision=HIGH) + proj_bias
    normed_mlp = low(layer_norm(tokens, mlp_gain, mlp_shift))
    before = low_back(jnp.dot(normed_mlp, up_weight, precision=HIGH) + up_bias)
    activated = low(gelu_exact(before))
    branch_mlp = jnp.dot(activated, down_weight, precision=HIGH) + down_bias
    return tokens + branch_attn + branch_mlp

def reference(tokens, segments, attn_gain, attn_shift, qkv_weight, qkv_bias, proj_weight, proj_bias, mlp_gain, mlp_shift, up_weight, up_bias, down_weight, down_bias, cotangent):
    cosine, sine = rotary_tables(segments)
    cosine = cosine.reshape(TOKENS, 1, ROT)
    sine = sine.reshape(TOKENS, 1, ROT)
    weights_list = [piece.astype(jnp.float32) for piece in (attn_gain, attn_shift, qkv_weight, qkv_bias, proj_weight, proj_bias, mlp_gain, mlp_shift, up_weight, up_bias, down_weight, down_bias)]

    def forward_pass(inputs, *weights):
        return block(inputs, *weights, cosine, sine, segments)
    output, pullback = jax.vjp(forward_pass, tokens.astype(jnp.float32), *weights_list)
    gradients = pullback(cotangent.astype(jnp.float32))
    return (output.astype(jnp.bfloat16), gradients[0], gradients[1], gradients[2], gradients[3], gradients[4], gradients[5], gradients[6], gradients[7], gradients[8], gradients[9], gradients[10], gradients[11], gradients[12])
```

```python
import math

import jax
import jax.numpy as jnp
from jax import lax
from jax.experimental import pallas as pl
from jax.experimental.pallas import tpu as pltpu
from jax.sharding import Mesh
from jax.sharding import PartitionSpec as P

D = 768
HEADS = 12
HEAD_DIM = 64
ROT = 16
BLK = 256
PAIR = 2 * HEAD_DIM
SPAN = 3
EPS = 1e-05
F32 = jnp.float32
BF16 = jnp.bfloat16
REP = ("rep_hi", "rep_lo")


def dot_nt(left, right):
    return lax.dot_general(left, right, (((1,), (1,)), ((), ())), preferred_element_type=F32)


def dot_nn(left, right):
    return lax.dot_general(left, right, (((1,), (0,)), ((), ())), preferred_element_type=F32)


def dot_tn(left, right):
    return lax.dot_general(left, right, (((0,), (0,)), ((), ())), preferred_element_type=F32)


def attention_kernel(
    first_ref, q_ref, k_ref, v_ref, grad_ref, cos_ref, up_ref, down_ref, start_ref,
    out_ref, back_ref, qs, ks, vs, kt, vt, dk, dv,
):
    length = q_ref.shape[0]
    half = ROT // 2
    scale = HEAD_DIM ** -0.5

    def turn(x):
        return (
            x * cos_ref[...]
            + pltpu.roll(x, PAIR - half, 1) * up_ref[...]
            + pltpu.roll(x, half, 1) * down_ref[...]
        )

    def turn_back(g, rows):
        return (
            g * cos_ref[rows, :]
            + pltpu.roll(g * up_ref[rows, :], half, 1)
            + pltpu.roll(g * down_ref[rows, :], PAIR - half, 1)
        )

    qs[...] = turn(q_ref[...]).astype(BF16)
    keys = turn(k_ref[...]).astype(BF16)
    ks[...] = keys
    kt[...] = keys.astype(F32).T.astype(BF16)
    values = v_ref[...].astype(BF16)
    vs[...] = values
    vt[...] = values.astype(F32).T.astype(BF16)
    dk[...] = jnp.zeros_like(dk)
    dv[...] = jnp.zeros_like(dv)
    low = lax.broadcasted_iota(jnp.int32, (BLK, PAIR), 1) < HEAD_DIM

    def block(at, count):
        extent = count * BLK
        query_at = pl.multiple_of(at * BLK, BLK)
        key_at = pl.multiple_of((at - count + 1) * BLK, BLK)
        rows = pl.ds(query_at, BLK)
        cols = pl.ds(key_at, extent)
        qb = qs[rows, :]
        gb = grad_ref[rows, :]
        kb = ks[cols, :]
        vb = vs[cols, :]
        start = start_ref[:, rows]
        key_index = lax.broadcasted_iota(jnp.int32, (extent, BLK), 0)
        query_index = lax.broadcasted_iota(jnp.int32, (extent, BLK), 1) + (count - 1) * BLK
        allowed = (key_index >= start - key_at) & (key_index <= query_index)
        outs, dqs = [], []
        dk_new = dv_new = None
        for head in range(2):
            lanes = low if head == 0 else ~low
            part = slice(head * HEAD_DIM, (head + 1) * HEAD_DIM)
            qh = jnp.where(lanes, qb, jnp.zeros_like(qb))
            gh = jnp.where(lanes, gb, jnp.zeros_like(gb))
            scores = jnp.where(allowed, dot_nt(kb, qh) * (scale * math.log2(math.e)), -1e30)
            weight = jnp.exp2(scores - jnp.max(scores, axis=0, keepdims=True))
            probs = weight * (1.0 / jnp.sum(weight, axis=0, keepdims=True))
            low_probs = probs.astype(BF16)
            outs.append(dot_nn(vt[part, cols], low_probs))
            grad_probs = dot_nt(vb, gh)
            delta = jnp.sum(probs * grad_probs, axis=0, keepdims=True)
            grad_scores = (probs * (grad_probs - delta)).astype(BF16)
            dqs.append(dot_nn(kt[part, cols], grad_scores))
            dv_part = dot_nn(low_probs, gh)
            dk_part = dot_nn(grad_scores, qh)
            dv_new = dv_part if dv_new is None else dv_new + dv_part
            dk_new = dk_part if dk_new is None else dk_new + dk_part
        dv[cols, :] += dv_new
        dk[cols, :] += dk_new
        out_ref[rows, :] = jnp.concatenate(outs, 0).T.astype(BF16)
        back_ref[0, rows, :] = turn_back(jnp.concatenate(dqs, 0).T * scale, rows).astype(BF16)

    def step(at, carry):
        needed = at - first_ref[at] + 1
        for count in range(1, SPAN + 1):
            pl.when(needed == count)(lambda count=count: block(at, count))
        return carry

    lax.fori_loop(0, length // BLK, step, 0)
    back_ref[1] = turn_back(dk[...] * scale, slice(None)).astype(BF16)
    back_ref[2] = dv[...].astype(BF16)


def attention(mixed, grad_heads, tables, start, first, pairs):
    length = mixed.shape[0]
    wide = mixed.shape[1] // 3 // PAIR
    first_block = start[0, ::BLK] // BLK

    def column(offset):
        return pl.BlockSpec((length, PAIR), lambda pair, _: (0, offset + pair))

    whole = pl.BlockSpec((length, PAIR), lambda pair, _: (0, 0))
    return pl.pallas_call(
        attention_kernel,
        grid_spec=pltpu.PrefetchScalarGridSpec(
            num_scalar_prefetch=1,
            grid=(pairs,),
            in_specs=[
                column(first), column(wide + first), column(2 * wide + first), column(first),
                whole, whole, whole, pl.BlockSpec((1, length), lambda pair, _: (0, 0)),
            ],
            out_specs=[column(0), pl.BlockSpec((3, length, PAIR), lambda pair, _: (0, 0, pair))],
            scratch_shapes=[pltpu.VMEM((length, PAIR), BF16)] * 3
            + [pltpu.VMEM((PAIR, length), BF16)] * 2
            + [pltpu.VMEM((length, PAIR), F32)] * 2,
        ),
        out_shape=[
            jax.ShapeDtypeStruct((length, pairs * PAIR), BF16),
            jax.ShapeDtypeStruct((3, length, pairs * PAIR), BF16),
        ],
        compiler_params=pltpu.CompilerParams(vmem_limit_bytes=40 * 1024 * 1024),
        cost_estimate=pl.CostEstimate(
            flops=pairs * 12 * length * 640 * HEAD_DIM * 12,
            bytes_accessed=pairs * length * PAIR * 24,
            transcendentals=pairs * 2 * length * 640,
        ),
        name="attention",
    )(first_block, mixed, mixed, mixed, grad_heads, *tables, start)


def rotary_tables(segments):
    length = segments.shape[1]
    half = ROT // 2
    position = jnp.arange(length, dtype=jnp.int32)[None]
    change = jnp.concatenate(
        [jnp.ones((1, 1), dtype=bool), segments[:, 1:] != segments[:, :-1]], axis=1
    )
    start = lax.cummax(jnp.where(change, position, 0), axis=1)
    place = (position - start).astype(F32)
    frequency = 10000.0 ** (-2.0 * jnp.arange(half, dtype=F32) / ROT)
    angles = place[0][:, None] * frequency
    cosine, sine = jnp.cos(angles), jnp.sin(angles)
    rest = HEAD_DIM - ROT
    zero = jnp.zeros((length, half), F32)
    zeros = jnp.zeros((length, rest), F32)
    tables = (
        jnp.concatenate([cosine, cosine, jnp.ones((length, rest), F32)], axis=1),
        jnp.concatenate([-sine, zero, zeros], axis=1),
        jnp.concatenate([zero, sine, zeros], axis=1),
    )
    return start, [jnp.tile(table, (1, 2)) for table in tables]


def gather_rows(weight):
    parts = lax.axis_size("rep_lo")
    rows = weight.shape[0] // parts
    own = lax.dynamic_slice_in_dim(weight, lax.axis_index("rep_lo") * rows, rows, axis=0)
    return lax.all_gather(own, ("shard", "rep_lo"), axis=0, tiled=True)


def swap(value, axis, mask):
    size = lax.axis_size(axis)
    return lax.ppermute(value, axis, [(i, i ^ mask) for i in range(size)])


def reduce_plan():
    rep_masks = [1 << i for i in range(lax.axis_size(REP).bit_length() - 1)]
    shard_masks = [1 << i for i in reversed(range(lax.axis_size("shard").bit_length() - 1))]
    return rep_masks, shard_masks


def halve(parts, axis, mask, at):
    bit = (lax.axis_index(axis) // mask) % 2
    send = lax.dynamic_index_in_dim(parts, 1 - bit, axis=at, keepdims=False)
    keep = lax.dynamic_index_in_dim(parts, bit, axis=at, keepdims=False)
    return (keep.astype(F32) + swap(send, axis, mask).astype(F32)).astype(BF16)


def double(part, axis, mask):
    bit = (lax.axis_index(axis) // mask) % 2
    other = swap(part, axis, mask)
    return jnp.where(bit == 1, jnp.stack([other, part]), jnp.stack([part, other]))


def sum_owned(grad):
    rows, cols = grad.shape
    rep_masks, shard_masks = reduce_plan()
    shards = lax.axis_size("shard")
    reps = lax.axis_size(REP)
    piece = rows // shards // reps
    parts = halve(grad.reshape(shards, 2, rows // shards // 2, cols), REP, rep_masks[0], 1)
    for mask in shard_masks:
        left = parts.shape[0] // 2
        parts = halve(parts.reshape(2, left, *parts.shape[1:]), "shard", mask, 0)
    parts = parts.reshape(-1, cols)
    for mask in rep_masks[1:]:
        parts = halve(parts.reshape(2, -1, cols), REP, mask, 0)
    for mask in reversed(rep_masks):
        parts = double(parts, REP, mask).reshape(-1, cols)
    return parts.astype(F32)


def shards(
    tokens, segments, attn_gain, attn_shift, qkv_weight, qkv_bias, proj_weight, proj_bias,
    mlp_gain, mlp_shift, up_weight, up_bias, down_weight, down_bias, cotangent,
):
    small = [attn_gain, attn_shift, qkv_bias, proj_bias, mlp_gain, mlp_shift, up_bias, down_bias]
    sizes = [vector.shape[0] for vector in small]
    edges = [sum(sizes[:i]) for i in range(len(sizes) + 1)]
    small_all = lax.all_gather(jnp.concatenate(small)[None], "shard", axis=0, tiled=True)
    gain_one, shift_one, mix_bias, out_bias, gain_two, shift_two, rise_bias, fall_bias = [
        small_all[:, a:b].reshape(-1).astype(F32) for a, b in zip(edges[:-1], edges[1:])
    ]
    rise = gather_rows(up_weight)
    fall = gather_rows(down_weight)
    mix = gather_rows(qkv_weight)
    out = gather_rows(proj_weight)

    inputs = tokens.astype(F32)
    length = inputs.shape[0]
    start, tables = rotary_tables(segments)
    center = inputs - jnp.mean(inputs, axis=-1, keepdims=True)
    inverse = lax.rsqrt(jnp.mean(center * center, axis=-1, keepdims=True) + EPS)
    unit = center * inverse
    low_one = (unit * gain_one + shift_one).astype(BF16)
    low_two = (unit * gain_two + shift_two).astype(BF16)
    upstream = cotangent.astype(F32)

    before = dot_nn(low_two, rise) + rise_bias
    chance = 0.5 * (1.0 + lax.erf(before * (1.0 / math.sqrt(2.0))))
    low_act = (before * chance).astype(BF16)
    branch_mlp = dot_nn(low_act, fall) + fall_bias
    grad_fall = dot_tn(low_act, cotangent).astype(BF16)
    slope = chance + before * jnp.exp(-0.5 * before * before) * (1.0 / math.sqrt(2.0 * math.pi))
    grad_before = (dot_nt(cotangent, fall) * slope).astype(BF16)
    grad_rise = dot_tn(low_two, grad_before).astype(BF16)
    rise_total = jnp.sum(grad_before.astype(F32), axis=0)
    error_two = dot_nt(grad_before, rise)

    mixed = dot_nn(low_one, mix) + mix_bias
    grad_heads = dot_nt(cotangent, out).astype(BF16)
    heads, back = attention(mixed, grad_heads, tables, start, 0, HEADS // 2)
    branch_attn = dot_nn(heads, out) + out_bias
    result = (inputs + branch_attn + branch_mlp).astype(BF16)
    grad_out = dot_tn(heads, cotangent).astype(BF16)
    grad_mix = jnp.concatenate([dot_tn(low_one, back[i]) for i in range(3)], axis=1).astype(BF16)
    mix_total = jnp.sum(back.astype(F32), axis=1).reshape(-1)
    error_one = sum(dot_nt(back[i], mix[:, i * D : (i + 1) * D]) for i in range(3))

    def norm_back(error, gain):
        scaled = error * gain
        return inverse * (
            scaled
            - jnp.mean(scaled, axis=-1, keepdims=True)
            - unit * jnp.mean(scaled * unit, axis=-1, keepdims=True)
        )

    tokens_grad = upstream + norm_back(error_one, gain_one) + norm_back(error_two, gain_two)
    upstream_total = jnp.sum(upstream, axis=0)
    totals = [
        jnp.sum(error_one * unit, axis=0), jnp.sum(error_one, axis=0), mix_total, upstream_total,
        jnp.sum(error_two * unit, axis=0), jnp.sum(error_two, axis=0), rise_total,
    ]
    count = lax.axis_size("shard")
    owned = jnp.concatenate([t.reshape(count, -1) for t in totals], axis=1).astype(BF16)
    owned = lax.psum(owned, (*REP, "shard"))
    owned = lax.dynamic_index_in_dim(owned, lax.axis_index("shard"), 0, keepdims=False).astype(F32)
    own = [owned[a:b] for a, b in zip(edges[:-2], edges[1:-1])]

    sum_fall = sum_owned(grad_fall)
    sum_rise = sum_owned(grad_rise)
    sum_last = sum_owned(jnp.concatenate([grad_mix, grad_out], axis=1))
    sum_mix, sum_out = sum_last[:, : 3 * D], sum_last[:, 3 * D :]
    return (
        result, tokens_grad, own[0], own[1], sum_mix, own[2], sum_out, own[3],
        own[4], own[5], sum_rise, own[6], sum_fall, own[3],
    )


def solution(mesh):
    reps, count = mesh.devices.shape
    fine = Mesh(mesh.devices.reshape(reps // 4, 4, count), (*REP, "shard"))
    rows = P((*REP, "shard"), None)
    line = P("shard")
    wide = P("shard", None)
    in_specs = (
        rows, rows, line, line, wide, line, wide, line, line, line, wide, line, wide, line, rows,
    )
    out_specs = (
        rows, rows, line, line, wide, line, wide, line, line, line, wide, line, wide, line,
    )
    return jax.shard_map(shards, mesh=fine, in_specs=in_specs, out_specs=out_specs, check_vma=False)
```

```python
import math

import jax
import jax.numpy as jnp
from jax import lax
from jax.experimental import pallas as pl
from jax.experimental.pallas import tpu as pltpu
from jax.sharding import Mesh
from jax.sharding import PartitionSpec as P

D = 768
HEADS = 12
HEAD_DIM = 64
ROT = 16
BLK = 256
PAIR = 2 * HEAD_DIM
PAIRS = HEADS // 2
SPAN = 3
EPS = 1e-05
F32 = jnp.float32
BF16 = jnp.bfloat16
REP = ("z", "x", "c")
VMEM_LIMIT = 56 * 1024 * 1024


def dot_nt(left, right):
    return lax.dot_general(left, right, (((1,), (1,)), ((), ())), preferred_element_type=F32)


def dot_nn(left, right):
    return lax.dot_general(left, right, (((1,), (0,)), ((), ())), preferred_element_type=F32)


def dot_tn(left, right):
    return lax.dot_general(left, right, (((0,), (0,)), ((), ())), preferred_element_type=F32)


def mlp_kernel(
    low_ref, low_t_ref, cot_ref, rise_ref, bias_ref, fall_ref, *rest, per_shard, count,
):
    act_ref, back_ref, grads_ref, total_ref, slope = rest[-5:]
    at = pl.program_id(0)
    tile = rise_ref.shape[1]
    before = dot_nn(low_ref[...], rise_ref[...]) + bias_ref[...]
    chance = 0.5 + 0.5 * lax.erf(before * (1.0 / math.sqrt(2.0)))
    slope[...] = chance + before * jnp.exp(-0.5 * before * before) * (1.0 / math.sqrt(2.0 * math.pi))
    act_ref[...] = (before * chance).astype(BF16)
    grad_fall = dot_tn(act_ref[...], cot_ref[...]).astype(BF16)
    owner_fall = at // per_shard
    place = pl.ds(pl.multiple_of(lax.rem(at, per_shard) * tile, tile), tile)
    grads_ref[owner_fall, 0, place, :] = grad_fall
    back_ref[...] = (dot_nt(cot_ref[...], fall_ref[...]) * slope[...]).astype(BF16)
    low_grad = back_ref[...]
    total_ref[...] = jnp.sum(low_grad.astype(F32), axis=0, keepdims=True)
    grad_rise = dot_nn(low_t_ref[...], low_grad).astype(BF16)
    rows = D // count
    wide = D // tile
    block = at // wide
    cols = pl.ds(pl.multiple_of(lax.rem(at, wide) * tile, tile), tile)
    for owner in range(count):
        at_rows = pl.ds(pl.multiple_of(block * rows, rows), rows)
        grads_ref[owner, 1, at_rows, cols] = grad_rise[owner * rows : (owner + 1) * rows, :]


def mlp(low, low_t, cot, rise, bias, fall, waits):
    length = low.shape[0]
    hidden = rise.shape[1]
    count = lax.axis_size("shard")
    width = hidden // count
    tile = 256 if width % 256 == 0 else 128
    whole = pl.BlockSpec((length, D), lambda at: (0, 0))
    column = pl.BlockSpec((length, tile), lambda at: (0, at))
    line = pl.BlockSpec((1, tile), lambda at: (0, at))
    return pl.pallas_call(
        lambda *refs: mlp_kernel(*refs, per_shard=width // tile, count=count),
        grid=(hidden // tile,),
        in_specs=[
            whole,
            pl.BlockSpec((D, length), lambda at: (0, 0)),
            whole,
            pl.BlockSpec((D, tile), lambda at: (0, at)),
            line,
            pl.BlockSpec((tile, D), lambda at: (at, 0)),
        ]
        + [pl.BlockSpec(memory_space=pl.ANY)] * len(waits),
        out_specs=[
            column,
            column,
            pl.BlockSpec((count, 2, width, D), lambda at: (0, 0, 0, 0)),
            line,
        ],
        out_shape=[
            jax.ShapeDtypeStruct((length, hidden), BF16),
            jax.ShapeDtypeStruct((length, hidden), BF16),
            jax.ShapeDtypeStruct((count, 2, width, D), BF16),
            jax.ShapeDtypeStruct((1, hidden), F32),
        ],
        scratch_shapes=[pltpu.VMEM((length, tile), F32)],
        compiler_params=pltpu.CompilerParams(vmem_limit_bytes=VMEM_LIMIT),
        cost_estimate=pl.CostEstimate(
            flops=8 * length * D * hidden,
            bytes_accessed=6 * length * D + 8 * D * hidden + 4 * length * hidden,
            transcendentals=2 * length * hidden,
        ),
        name="mlp",
    )(low, low_t, cot, rise, bias, fall, *waits)


def attention_kernel(
    first_ref, low_ref, low_t_ref, cot_ref, wq_ref, wk_ref, wv_ref, bq_ref, bk_ref, bv_ref, out_w_ref,
    cos_ref, up_ref, down_ref, start_ref, *rest, each, count,
):
    (
        ob, back, grads_ref, grad_out_ref, total_ref, qs, ks, vs, kt, vt, dk, dv, gs, ot, w3,
    ) = rest[-15:]
    length = low_ref.shape[0]
    half = ROT // 2
    scale = HEAD_DIM ** -0.5

    def turn(x):
        return (
            x * cos_ref[...]
            + pltpu.roll(x, PAIR - half, 1) * up_ref[...]
            + pltpu.roll(x, half, 1) * down_ref[...]
        )

    def turn_back(g, rows):
        return (
            g * cos_ref[rows, :]
            + pltpu.roll(g * up_ref[rows, :], half, 1)
            + pltpu.roll(g * down_ref[rows, :], PAIR - half, 1)
        )

    w3[:, :PAIR] = wq_ref[...]
    w3[:, PAIR : 2 * PAIR] = wk_ref[...]
    w3[:, 2 * PAIR :] = wv_ref[...]
    mixed = dot_nn(low_ref[...], w3[...])
    qs[...] = turn(mixed[:, :PAIR] + bq_ref[...]).astype(BF16)
    keys = turn(mixed[:, PAIR : 2 * PAIR] + bk_ref[...]).astype(BF16)
    ks[...] = keys
    kt[...] = keys.astype(F32).T.astype(BF16)
    values = (mixed[:, 2 * PAIR :] + bv_ref[...]).astype(BF16)
    vs[...] = values
    vt[...] = values.astype(F32).T.astype(BF16)
    gs[...] = dot_nt(cot_ref[...], out_w_ref[...]).astype(BF16)
    dk[...] = jnp.zeros_like(dk)
    dv[...] = jnp.zeros_like(dv)
    low = lax.broadcasted_iota(jnp.int32, (BLK, PAIR), 1) < HEAD_DIM

    def block(at, blocks):
        extent = blocks * BLK
        query_at = pl.multiple_of(at * BLK, BLK)
        key_at = pl.multiple_of((at - blocks + 1) * BLK, BLK)
        rows = pl.ds(query_at, BLK)
        cols = pl.ds(key_at, extent)
        qb = qs[rows, :]
        gb = gs[rows, :]
        kb = ks[cols, :]
        vb = vs[cols, :]
        start = start_ref[:, rows]
        key_index = lax.broadcasted_iota(jnp.int32, (extent, BLK), 0)
        query_index = lax.broadcasted_iota(jnp.int32, (extent, BLK), 1) + (blocks - 1) * BLK
        allowed = (key_index >= start - key_at) & (key_index <= query_index)
        outs, dqs = [], []
        dk_new = dv_new = None
        for head in range(2):
            lanes = low if head == 0 else ~low
            part = slice(head * HEAD_DIM, (head + 1) * HEAD_DIM)
            qh = jnp.where(lanes, qb, jnp.zeros_like(qb))
            gh = jnp.where(lanes, gb, jnp.zeros_like(gb))
            scores = jnp.where(allowed, dot_nt(kb, qh) * (scale * math.log2(math.e)), -1e30)
            weight = jnp.exp2(scores - jnp.max(scores, axis=0, keepdims=True))
            probs = weight * (1.0 / jnp.sum(weight, axis=0, keepdims=True))
            low_probs = probs.astype(BF16)
            outs.append(dot_nn(vt[part, cols], low_probs))
            grad_probs = dot_nt(vb, gh)
            delta = jnp.sum(probs * grad_probs, axis=0, keepdims=True)
            grad_scores = (probs * (grad_probs - delta)).astype(BF16)
            dqs.append(dot_nn(kt[part, cols], grad_scores))
            dv_part = dot_nn(low_probs, gh)
            dk_part = dot_nn(grad_scores, qh)
            dv_new = dv_part if dv_new is None else dv_new + dv_part
            dk_new = dk_part if dk_new is None else dk_new + dk_part
        dv[cols, :] += dv_new
        dk[cols, :] += dk_new
        out_t = jnp.concatenate(outs, 0)
        ot[:, rows] = out_t.astype(BF16)
        ob[rows, :] = out_t.T.astype(BF16)
        back[0, rows, :] = turn_back(jnp.concatenate(dqs, 0).T * scale, rows).astype(BF16)

    def step(at, carry):
        needed = at - first_ref[at] + 1
        for blocks in range(1, SPAN + 1):
            pl.when(needed == blocks)(lambda blocks=blocks: block(at, blocks))
        return carry

    lax.fori_loop(0, length // BLK, step, 0)
    back[1] = turn_back(dk[...] * scale, slice(None)).astype(BF16)
    back[2] = dv[...].astype(BF16)
    grad_mixed = jnp.concatenate([back[0], back[1], back[2]], axis=1)
    total_ref[...] = jnp.sum(grad_mixed.astype(F32), axis=0, keepdims=True)
    grad_w = dot_nn(low_t_ref[...], grad_mixed).astype(BF16)
    grad_out = dot_nn(ot[...], cot_ref[...]).astype(BF16)
    grad_out_ref[...] = grad_out
    at = pl.program_id(0)
    rows = D // count
    split = grads_ref.shape[2]
    cols = pl.ds(pl.multiple_of(at * 3 * PAIR, PAIR), 3 * PAIR)
    for owner in range(count):
        own = grad_w[owner * rows : (owner + 1) * rows, :]
        grads_ref[0, owner, :, cols] = own[:split]
        grads_ref[1, owner, : rows - split, cols] = own[split:]
    if 2 * split > rows:
        cols = pl.ds(pl.multiple_of(lax.rem(at, each) * D, D), D)
        grads_ref[1, at // each, rows - split :, cols] = grad_out


def attention(low, low_t, cot, both, mix_bias, tables, start, first, each, shared, waits):
    length = low.shape[0]
    count = lax.axis_size("shard")
    first_block = start[0, ::BLK] // BLK
    rows = D // count
    joint = count == 2

    def pair(at):
        return at // each * (PAIRS // 2) + first + at % each

    def weight(offset):
        return pl.BlockSpec((D, PAIR), lambda at, _: (0, offset + pair(at)))

    def bias(offset):
        return pl.BlockSpec((1, PAIR), lambda at, _: (0, offset + pair(at)))

    def fixed(*shape):
        return pl.BlockSpec(shape, lambda at, _: (0,) * len(shape))

    pairs = 2 * each
    grads = (2, count, (rows + (PAIR if joint else 0)) // 2, pairs * 3 * PAIR)
    return pl.pallas_call(
        lambda *refs: attention_kernel(*refs, each=each, count=count),
        grid_spec=pltpu.PrefetchScalarGridSpec(
            num_scalar_prefetch=1,
            grid=(pairs,),
            in_specs=[
                fixed(length, D), fixed(D, length), fixed(length, D),
                weight(0), weight(PAIRS), weight(2 * PAIRS),
                bias(0), bias(PAIRS), bias(2 * PAIRS),
                pl.BlockSpec((PAIR, D), lambda at, _: (pair(at), 3)),
                fixed(length, PAIR), fixed(length, PAIR), fixed(length, PAIR), fixed(1, length),
            ]
            + [pl.BlockSpec(memory_space=pl.ANY)] * len((*shared, *waits)),
            out_specs=[
                pl.BlockSpec((length, PAIR), lambda at, _: (0, pair(at))),
                pl.BlockSpec((3, length, PAIR), lambda at, _: (0, 0, pair(at))),
                fixed(*grads),
                pl.BlockSpec((PAIR, D), lambda at, _: (at, 0)),
                pl.BlockSpec((1, 3 * PAIR), lambda at, _: (0, pair(at))),
            ],
            scratch_shapes=[pltpu.VMEM((length, PAIR), BF16)] * 3
            + [pltpu.VMEM((PAIR, length), BF16)] * 2
            + [pltpu.VMEM((length, PAIR), F32)] * 2
            + [
                pltpu.VMEM((length, PAIR), BF16), pltpu.VMEM((PAIR, length), BF16),
                pltpu.VMEM((D, 3 * PAIR), BF16),
            ],
        ),
        out_shape=[
            jax.ShapeDtypeStruct((length, D), BF16),
            jax.ShapeDtypeStruct((3, length, D), BF16),
            jax.ShapeDtypeStruct(grads, BF16),
            jax.ShapeDtypeStruct((pairs * PAIR, D), BF16),
            jax.ShapeDtypeStruct((1, 3 * D), F32),
        ],
        compiler_params=pltpu.CompilerParams(vmem_limit_bytes=VMEM_LIMIT),
        cost_estimate=pl.CostEstimate(
            flops=pairs * (20 * length * D * PAIR + 12 * length * 640 * HEAD_DIM * 16),
            bytes_accessed=6 * length * D + pairs * (D * PAIR * 16 + length * PAIR * 8),
            transcendentals=pairs * 2 * length * 640,
        ),
        input_output_aliases=dict(zip((15, 16, 17), (0, 1, 4))) if shared else {},
        name="attention",
    )(
        first_block, low, low_t, cot, both, both, both, mix_bias, mix_bias, mix_bias, both, *tables,
        start, *shared, *waits,
    )


def errors_kernel(
    grad_ref, rise_ref, back_ref, both_ref, tokens_ref, cot_ref, gain_one_ref, gain_two_ref, *rest,
):
    out_ref, sums_ref = rest[-2:]
    inputs = tokens_ref[...].astype(F32)
    upstream = cot_ref[...].astype(F32)
    center = inputs - jnp.mean(inputs, axis=-1, keepdims=True)
    inverse = lax.rsqrt(jnp.mean(center * center, axis=-1, keepdims=True) + EPS)
    unit = center * inverse
    error_two = dot_nt(grad_ref[...], rise_ref[...])
    error_one = dot_nt(back_ref[0], both_ref[:, :D])
    error_one += dot_nt(back_ref[1], both_ref[:, D : 2 * D])
    error_one += dot_nt(back_ref[2], both_ref[:, 2 * D :])
    total = upstream
    for error, gain_ref in ((error_one, gain_one_ref), (error_two, gain_two_ref)):
        scaled = error * gain_ref[...]
        total += inverse * (
            scaled
            - jnp.mean(scaled, axis=-1, keepdims=True)
            - unit * jnp.mean(scaled * unit, axis=-1, keepdims=True)
        )
    out_ref[...] = total
    sums = [error_one * unit, error_one, error_two * unit, error_two, upstream]

    @pl.when(pl.program_id(0) == 0)
    def _():
        sums_ref[...] = jnp.zeros_like(sums_ref)

    for row, value in enumerate(sums):
        sums_ref[row : row + 1, :] += jnp.sum(value, axis=0, keepdims=True)


def input_errors(grad, rise, back, both, tokens, cot, gain_one, gain_two, waits):
    length, hidden = grad.shape

    def rows(wide):
        return pl.BlockSpec((BLK, wide), lambda at: (at, 0))

    def fixed(*shape):
        return pl.BlockSpec(shape, lambda at: (0,) * len(shape))

    return pl.pallas_call(
        errors_kernel,
        grid=(length // BLK,),
        in_specs=[
            rows(hidden), fixed(D, hidden), pl.BlockSpec((3, BLK, D), lambda at: (0, at, 0)),
            fixed(D, 3 * D), rows(D), rows(D), fixed(1, D), fixed(1, D),
        ]
        + [pl.BlockSpec(memory_space=pl.ANY)] * len(waits),
        out_specs=[rows(D), fixed(8, D)],
        out_shape=[jax.ShapeDtypeStruct((length, D), F32), jax.ShapeDtypeStruct((8, D), F32)],
        compiler_params=pltpu.CompilerParams(vmem_limit_bytes=VMEM_LIMIT),
        cost_estimate=pl.CostEstimate(
            flops=2 * length * D * (hidden + 3 * D),
            bytes_accessed=2 * (length + D) * (hidden + 3 * D) + 8 * length * D,
            transcendentals=length,
        ),
        name="input_errors",
    )(grad, rise, back, both, tokens, cot, gain_one, gain_two, *waits)


def output_kernel(act_ref, fall_ref, heads_ref, out_w_ref, tokens_ref, bias_ref, *rest):
    branches = dot_nn(act_ref[...], fall_ref[...]) + dot_nn(heads_ref[...], out_w_ref[...])
    total = tokens_ref[...].astype(F32) + branches + bias_ref[...]
    rest[-1][...] = total.astype(BF16)


def block_output(act, fall, heads, both, tokens, bias, waits):
    length, hidden = act.shape

    def rows(wide):
        return pl.BlockSpec((BLK, wide), lambda at: (at, 0))

    return pl.pallas_call(
        output_kernel,
        grid=(length // BLK,),
        in_specs=[
            rows(hidden), pl.BlockSpec((hidden, D), lambda at: (0, 0)), rows(D),
            pl.BlockSpec((D, D), lambda at: (0, 3)), rows(D), pl.BlockSpec((1, D), lambda at: (0, 0)),
        ]
        + [pl.BlockSpec(memory_space=pl.ANY)] * len(waits),
        out_specs=rows(D),
        out_shape=jax.ShapeDtypeStruct((length, D), BF16),
        compiler_params=pltpu.CompilerParams(vmem_limit_bytes=VMEM_LIMIT),
        cost_estimate=pl.CostEstimate(
            flops=2 * length * D * (hidden + D),
            bytes_accessed=2 * (length + D) * (hidden + D) + 4 * length * D,
            transcendentals=0,
        ),
        name="block_output",
    )(act, fall, heads, both, tokens, bias, *waits)


def rotary_tables(segments):
    length = segments.shape[1]
    half = ROT // 2
    position = jnp.arange(length, dtype=jnp.int32)[None]
    change = jnp.concatenate(
        [jnp.ones((1, 1), dtype=bool), segments[:, 1:] != segments[:, :-1]], axis=1
    )
    start = lax.cummax(jnp.where(change, position, 0), axis=1)
    place = (position - start).astype(F32)
    frequency = 10000.0 ** (-2.0 * jnp.arange(half, dtype=F32) / ROT)
    angles = place[0][:, None] * frequency
    cosine, sine = jnp.cos(angles), jnp.sin(angles)
    rest = HEAD_DIM - ROT
    zero = jnp.zeros((length, half), F32)
    zeros = jnp.zeros((length, rest), F32)
    tables = (
        jnp.concatenate([cosine, cosine, jnp.ones((length, rest), F32)], axis=1),
        jnp.concatenate([-sine, zero, zeros], axis=1),
        jnp.concatenate([zero, sine, zeros], axis=1),
    )
    return start, [jnp.tile(table, (1, 2)) for table in tables]


def tie(value, *others):
    return lax.optimization_barrier((value, *others))[0]


def bit_of(axis, mask):
    return (lax.axis_index(axis) // mask) % 2


def swap(value, axis, mask):
    size = lax.axis_size(axis)
    return lax.ppermute(value, axis, [(i, i ^ mask) for i in range(size)])


def log2(size):
    return size.bit_length() - 1


class Chain:
    def __init__(self, steps):
        self.steps = steps
        self.result = None
        self.last = None

    def step(self, *after):
        if self.result is not None:
            return self.last
        try:
            self.last = next(self.steps) if self.last is None else self.steps.send(after)
        except StopIteration as stop:
            self.result = self.last = stop.value
        return self.last

    def finish(self, *after):
        while self.result is None:
            self.step(*after)
        return self.result


def arrived(value, after):
    return tie(value, *after) if after else value


def joined(mine, other, bit):
    return jnp.where(bit == 1, jnp.stack([other, mine]), jnp.stack([mine, other]))


def own_part(weight):
    parts = lax.axis_size("x") * lax.axis_size("c")
    rows = weight.shape[0] // parts
    at = lax.axis_index(("x", "c")) * rows
    return lax.dynamic_slice_in_dim(weight, at, rows, axis=0)


def gather_rows(weight):
    return lax.all_gather(own_part(weight), ("shard", "x", "c"), axis=0, tiled=True)


def gather_steps(weight, *after):
    other = own_part(weight)
    other = tie(other, *after) if after else other
    got = swap(other, "shard", 1)
    other = arrived(got, (yield other))
    for axis, at in (("x", 0), ("c", 1)):
        got = swap(other, axis, 1)
        got = arrived(got, (yield other))
        bit = lax.axis_index(axis)
        other = jnp.where(
            bit == 1, jnp.stack([got, other], at), jnp.stack([other, got], at)
        )
    other = other.reshape(weight.shape)
    return joined(weight, other, lax.axis_index("shard")).reshape(-1, weight.shape[1])


def sum_steps(grads):
    dims = [("c", 1)]
    dims += [("shard", 1 << i) for i in reversed(range(log2(lax.axis_size("shard"))))]
    rep = [("x", 1)] + [("z", 1 << i) for i in range(log2(lax.axis_size("z")))]
    parts = grads
    for dim in dims + rep:
        half = parts.reshape(2, -1, grads.shape[-1])
        bit = bit_of(*dim)
        send = lax.dynamic_index_in_dim(half, 1 - bit, axis=0, keepdims=False)
        got = swap(send, *dim)
        got = arrived(got, (yield send))
        keep = lax.dynamic_index_in_dim(half, bit, axis=0, keepdims=False)
        parts = (keep.astype(F32) + got.astype(F32)).astype(BF16)
    for dim in rep[::-1] + dims[:1]:
        got = swap(parts, *dim)
        got = arrived(got, (yield parts))
        parts = joined(parts, got, bit_of(*dim)).reshape(-1, grads.shape[-1])
    return parts.reshape(2, -1, grads.shape[-1])


def sum_offloaded(grads):
    parts = grads.reshape(-1, grads.shape[-1])
    parts = lax.psum_scatter(parts, ("shard", "c", "x"), scatter_dimension=0, tiled=True)
    parts = lax.psum_scatter(parts, "z", scatter_dimension=0, tiled=True)
    parts = lax.all_gather(parts, ("c", "x", "z"), axis=0, tiled=True)
    return parts.reshape(grads.shape[1:])


def total_steps(totals):
    rep = [("c", 1), ("x", 1)] + [("z", 1 << i) for i in range(log2(lax.axis_size("z")))]
    parts = totals
    for mask in [1 << i for i in reversed(range(log2(totals.shape[0])))]:
        half = parts.reshape(2, -1)
        bit = bit_of("shard", mask)
        send = lax.dynamic_index_in_dim(half, 1 - bit, axis=0, keepdims=False).astype(BF16)
        got = swap(send, "shard", mask)
        got = arrived(got, (yield send))
        parts = lax.dynamic_index_in_dim(half, bit, axis=0, keepdims=False) + got.astype(F32)
    for dim in rep:
        sent = parts.reshape(-1).astype(BF16)
        got = swap(sent, *dim)
        got = arrived(got, (yield sent))
        parts = sent.astype(F32) + got.astype(F32)
    return parts


def shards(
    tokens, segments, attn_gain, attn_shift, qkv_weight, qkv_bias, proj_weight, proj_bias,
    mlp_gain, mlp_shift, up_weight, up_bias, down_weight, down_bias, cotangent,
):
    count = lax.axis_size("shard")
    joint = count == 2
    small = [attn_gain, attn_shift, qkv_bias, proj_bias, mlp_gain, mlp_shift, up_bias, down_bias]
    sizes = [vector.shape[0] for vector in small]
    edges = [sum(sizes[:i]) for i in range(len(sizes) + 1)]
    own_small = jnp.concatenate(small)[None]
    own_both = jnp.concatenate([qkv_weight, proj_weight], axis=1)
    if joint:
        small_all = joined(own_small, swap(own_small, "shard", 1), lax.axis_index("shard"))
        small_all = small_all.reshape(2, -1)
        rise_chain, fall_chain, both_chain = [
            Chain(gather_steps(weight)) for weight in (up_weight, down_weight, own_both)
        ]
        rise_chain.step()
        mark = rise_chain.step()
        fall_chain.steps = gather_steps(down_weight, mark)
        fall_chain.step()
        rise_chain.step()
        mark = fall_chain.step()
        both_chain.steps = gather_steps(own_both, mark)
        both_chain.step()
        rise = rise_chain.finish()
        mark = fall_chain.step()
        both_chain.step(mark)
        fall = fall_chain.finish()
    else:
        small_all = lax.all_gather(own_small, "shard", axis=0, tiled=True)
        rise, fall, both = [gather_rows(w) for w in (up_weight, down_weight, own_both)]
    gain_one, shift_one, mix_bias, out_bias, gain_two, shift_two, rise_bias, fall_bias = [
        small_all[:, a:b].reshape(1, -1).astype(F32) for a, b in zip(edges[:-1], edges[1:])
    ]

    inputs = tokens.astype(F32)
    start, tables = rotary_tables(segments)
    center = inputs - jnp.mean(inputs, axis=-1, keepdims=True)
    inverse = lax.rsqrt(jnp.mean(center * center, axis=-1, keepdims=True) + EPS)
    unit = center * inverse
    low_one = (unit * gain_one + shift_one).astype(BF16)
    low_two = (unit * gain_two + shift_two).astype(BF16)
    low_one_t = low_one.T
    low_two_t = low_two.T
    rows = D // count
    each = (2, 1)
    waits = (both_chain.last,) if joint else ()
    act, act_back, mlp_grads, rise_total = mlp(
        low_two, low_two_t, cotangent, rise, rise_bias, fall, waits
    )
    mlp_own = sum_offloaded(mlp_grads)
    if joint:
        both_chain.step(rise_total)
        both = both_chain.finish()

    def attend(first, each, shared, *waits):
        return attention(
            low_one, low_one_t, cotangent, both, mix_bias, tables, start, first, each, shared, waits
        )

    out_a, back_a, grads_a, grad_out_a, total_a = attend(0, each[0], (), rise_total)
    sum_a = Chain(sum_steps(grads_a))
    sum_a.step()
    sent = sum_a.step()
    heads, back, grads_b, grad_out_b, mix_total = attend(
        each[0], each[1], (out_a, back_a, total_a), sent
    )
    sum_b = Chain(sum_steps(grads_b))
    marks = [sum_b.step(), sum_a.step(mix_total)]
    tokens_grad, sums = input_errors(
        act_back, rise, back, both, tokens, cotangent, gain_one, gain_two, marks
    )
    mix_total = mix_total.reshape(PAIRS, 3, PAIR).swapaxes(0, 1)
    totals = [sums[0], sums[1], mix_total, sums[4], sums[2], sums[3], rise_total]
    totals = jnp.concatenate([t.reshape(count, -1) for t in totals], axis=1)
    total_chain = Chain(total_steps(totals))
    marks = [total_chain.step(), sum_b.step(sums), sum_a.step(sums)]
    result = block_output(act, fall, heads, both, tokens, out_bias + fall_bias, marks)
    owned = total_chain.finish()
    mix_own = [sum_a.finish(), sum_b.finish()]
    own = [owned[a:b] for a, b in zip(edges[:-2], edges[1:-1])]

    sum_fall = mlp_own[0].astype(F32)
    blocks = mlp_own[1].reshape(-1, rows, D)
    sum_rise = jnp.concatenate(list(blocks), axis=1).astype(F32)
    mix_own = [own.reshape(-1, own.shape[-1]) for own in mix_own]
    pair_rows = [own[:rows].reshape(rows, 2, n, 3, PAIR) for own, n in zip(mix_own, each)]
    sum_mix = jnp.concatenate(
        [
            part[:, half, at, kind]
            for kind in range(3)
            for half in range(2)
            for part, n in zip(pair_rows, each)
            for at in range(n)
        ],
        axis=1,
    ).astype(F32)
    if joint:
        blocks = [
            own[rows:, at * D : (at + 1) * D] for own, n in zip(mix_own, each) for at in range(n)
        ]
        sum_out = jnp.concatenate(blocks, axis=0).astype(F32)
    else:
        grads = [g.reshape(2, -1, D) for g in (grad_out_a, grad_out_b)]
        grads = jnp.concatenate(grads, axis=1).reshape(count, 2, rows // 2, D).swapaxes(0, 1)
        sum_out = Chain(sum_steps(grads)).finish().reshape(rows, D).astype(F32)
    return (
        result, tokens_grad, own[0], own[1], sum_mix, own[2], sum_out, own[3],
        own[4], own[5], sum_rise, own[6], sum_fall, own[3],
    )


def solution(mesh):
    reps, count = mesh.devices.shape
    fine = Mesh(mesh.devices.reshape(reps // 4, 2, 2, count), (*REP, "shard"))
    rows = P((*REP, "shard"), None)
    line = P("shard")
    wide = P("shard", None)
    in_specs = (
        rows, rows, line, line, wide, line, wide, line, line, line, wide, line, wide, line, rows,
    )
    out_specs = (
        rows, rows, line, line, wide, line, wide, line, line, line, wide, line, wide, line,
    )
    return jax.shard_map(shards, mesh=fine, in_specs=in_specs, out_specs=out_specs, check_vma=False)
```

```python
import math

import jax
import jax.numpy as jnp
from jax import lax
from jax.experimental import pallas as pl
from jax.experimental.pallas import tpu as pltpu
from jax.sharding import Mesh
from jax.sharding import PartitionSpec as P

D = 768
HEADS = 12
HEAD_DIM = 64
ROT = 16
BLK = 256
PAIR = 2 * HEAD_DIM
PAIRS = HEADS // 2
SPAN = 3
EPS = 1e-05
F32 = jnp.float32
BF16 = jnp.bfloat16
REP = ("z", "x", "c")
VMEM_LIMIT = 56 * 1024 * 1024


def dot_nt(left, right):
    return lax.dot_general(left, right, (((1,), (1,)), ((), ())), preferred_element_type=F32)


def dot_nn(left, right):
    return lax.dot_general(left, right, (((1,), (0,)), ((), ())), preferred_element_type=F32)


def dot_tn(left, right):
    return lax.dot_general(left, right, (((0,), (0,)), ((), ())), preferred_element_type=F32)


def mlp_kernel(
    low_ref, low_t_ref, cot_ref, rise_ref, bias_ref, fall_ref, *rest, per_shard, count,
):
    act_ref, back_ref, grads_ref, total_ref, slope = rest[-5:]
    at = pl.program_id(0)
    tile = rise_ref.shape[1]
    before = dot_nn(low_ref[...], rise_ref[...]) + bias_ref[...]
    chance = 0.5 + 0.5 * lax.erf(before * (1.0 / math.sqrt(2.0)))
    slope[...] = chance + before * jnp.exp(-0.5 * before * before) * (1.0 / math.sqrt(2.0 * math.pi))
    act_ref[...] = (before * chance).astype(BF16)
    grad_fall = dot_tn(act_ref[...], cot_ref[...]).astype(BF16)
    owner_fall = at // per_shard
    place = pl.ds(pl.multiple_of(lax.rem(at, per_shard) * tile, tile), tile)
    grads_ref[owner_fall, 0, place, :] = grad_fall
    back_ref[...] = (dot_nt(cot_ref[...], fall_ref[...]) * slope[...]).astype(BF16)
    low_grad = back_ref[...]
    total_ref[...] = jnp.sum(low_grad.astype(F32), axis=0, keepdims=True)
    grad_rise = dot_nn(low_t_ref[...], low_grad).astype(BF16)
    rows = D // count
    wide = D // tile
    block = at // wide
    cols = pl.ds(pl.multiple_of(lax.rem(at, wide) * tile, tile), tile)
    for owner in range(count):
        at_rows = pl.ds(pl.multiple_of(block * rows, rows), rows)
        grads_ref[owner, 1, at_rows, cols] = grad_rise[owner * rows : (owner + 1) * rows, :]


def mlp(low, low_t, cot, rise, bias, fall, waits):
    length = low.shape[0]
    hidden = rise.shape[1]
    count = lax.axis_size("shard")
    width = hidden // count
    tile = 256 if width % 256 == 0 else 128
    whole = pl.BlockSpec((length, D), lambda at: (0, 0))
    column = pl.BlockSpec((length, tile), lambda at: (0, at))
    line = pl.BlockSpec((1, tile), lambda at: (0, at))
    return pl.pallas_call(
        lambda *refs: mlp_kernel(*refs, per_shard=width // tile, count=count),
        grid=(hidden // tile,),
        in_specs=[
            whole,
            pl.BlockSpec((D, length), lambda at: (0, 0)),
            whole,
            pl.BlockSpec((D, tile), lambda at: (0, at)),
            line,
            pl.BlockSpec((tile, D), lambda at: (at, 0)),
        ]
        + [pl.BlockSpec(memory_space=pl.ANY)] * len(waits),
        out_specs=[
            column,
            column,
            pl.BlockSpec((count, 2, width, D), lambda at: (0, 0, 0, 0)),
            line,
        ],
        out_shape=[
            jax.ShapeDtypeStruct((length, hidden), BF16),
            jax.ShapeDtypeStruct((length, hidden), BF16),
            jax.ShapeDtypeStruct((count, 2, width, D), BF16),
            jax.ShapeDtypeStruct((1, hidden), F32),
        ],
        scratch_shapes=[pltpu.VMEM((length, tile), F32)],
        compiler_params=pltpu.CompilerParams(vmem_limit_bytes=VMEM_LIMIT),
        cost_estimate=pl.CostEstimate(
            flops=8 * length * D * hidden,
            bytes_accessed=6 * length * D + 8 * D * hidden + 4 * length * hidden,
            transcendentals=2 * length * hidden,
        ),
        name="mlp",
    )(low, low_t, cot, rise, bias, fall, *waits)


def attention_kernel(
    first_ref, low_ref, low_t_ref, cot_ref, wq_ref, wk_ref, wv_ref, bq_ref, bk_ref, bv_ref, out_w_ref,
    cos_ref, up_ref, down_ref, start_ref, *rest, each, count,
):
    (
        ob, back, grads_ref, grad_out_ref, total_ref, qs, ks, vs, kt, vt, dk, dv, gs, ot, w3,
    ) = rest[-15:]
    length = low_ref.shape[0]
    half = ROT // 2
    scale = HEAD_DIM ** -0.5

    def turn(x):
        return (
            x * cos_ref[...]
            + pltpu.roll(x, PAIR - half, 1) * up_ref[...]
            + pltpu.roll(x, half, 1) * down_ref[...]
        )

    def turn_back(g, rows):
        return (
            g * cos_ref[rows, :]
            + pltpu.roll(g * up_ref[rows, :], half, 1)
            + pltpu.roll(g * down_ref[rows, :], PAIR - half, 1)
        )

    w3[:, :PAIR] = wq_ref[...]
    w3[:, PAIR : 2 * PAIR] = wk_ref[...]
    w3[:, 2 * PAIR :] = wv_ref[...]
    mixed = dot_nn(low_ref[...], w3[...])
    qs[...] = turn(mixed[:, :PAIR] + bq_ref[...]).astype(BF16)
    keys = turn(mixed[:, PAIR : 2 * PAIR] + bk_ref[...]).astype(BF16)
    ks[...] = keys
    kt[...] = keys.astype(F32).T.astype(BF16)
    values = (mixed[:, 2 * PAIR :] + bv_ref[...]).astype(BF16)
    vs[...] = values
    vt[...] = values.astype(F32).T.astype(BF16)
    gs[...] = dot_nt(cot_ref[...], out_w_ref[...]).astype(BF16)
    dk[...] = jnp.zeros_like(dk)
    dv[...] = jnp.zeros_like(dv)
    low = lax.broadcasted_iota(jnp.int32, (BLK, PAIR), 1) < HEAD_DIM

    def block(at, blocks):
        extent = blocks * BLK
        query_at = pl.multiple_of(at * BLK, BLK)
        key_at = pl.multiple_of((at - blocks + 1) * BLK, BLK)
        rows = pl.ds(query_at, BLK)
        cols = pl.ds(key_at, extent)
        qb = qs[rows, :]
        gb = gs[rows, :]
        kb = ks[cols, :]
        vb = vs[cols, :]
        start = start_ref[:, rows]
        key_index = lax.broadcasted_iota(jnp.int32, (extent, BLK), 0)
        query_index = lax.broadcasted_iota(jnp.int32, (extent, BLK), 1) + (blocks - 1) * BLK
        allowed = (key_index >= start - key_at) & (key_index <= query_index)
        outs, dqs = [], []
        dk_new = dv_new = None
        for head in range(2):
            lanes = low if head == 0 else ~low
            part = slice(head * HEAD_DIM, (head + 1) * HEAD_DIM)
            qh = jnp.where(lanes, qb, jnp.zeros_like(qb))
            gh = jnp.where(lanes, gb, jnp.zeros_like(gb))
            scores = jnp.where(allowed, dot_nt(kb, qh) * (scale * math.log2(math.e)), -1e30)
            weight = jnp.exp2(scores - jnp.max(scores, axis=0, keepdims=True))
            probs = weight * (1.0 / jnp.sum(weight, axis=0, keepdims=True))
            low_probs = probs.astype(BF16)
            outs.append(dot_nn(vt[part, cols], low_probs))
            grad_probs = dot_nt(vb, gh)
            delta = jnp.sum(probs * grad_probs, axis=0, keepdims=True)
            grad_scores = (probs * (grad_probs - delta)).astype(BF16)
            dqs.append(dot_nn(kt[part, cols], grad_scores))
            dv_part = dot_nn(low_probs, gh)
            dk_part = dot_nn(grad_scores, qh)
            dv_new = dv_part if dv_new is None else dv_new + dv_part
            dk_new = dk_part if dk_new is None else dk_new + dk_part
        dv[cols, :] += dv_new
        dk[cols, :] += dk_new
        out_t = jnp.concatenate(outs, 0)
        ot[:, rows] = out_t.astype(BF16)
        ob[rows, :] = out_t.T.astype(BF16)
        back[0, rows, :] = turn_back(jnp.concatenate(dqs, 0).T * scale, rows).astype(BF16)

    def step(at, carry):
        needed = at - first_ref[at] + 1
        for blocks in range(1, SPAN + 1):
            pl.when(needed == blocks)(lambda blocks=blocks: block(at, blocks))
        return carry

    lax.fori_loop(0, length // BLK, step, 0)
    back[1] = turn_back(dk[...] * scale, slice(None)).astype(BF16)
    back[2] = dv[...].astype(BF16)
    grad_mixed = jnp.concatenate([back[0], back[1], back[2]], axis=1)
    total_ref[...] = jnp.sum(grad_mixed.astype(F32), axis=0, keepdims=True)
    grad_w = dot_nn(low_t_ref[...], grad_mixed).astype(BF16)
    grad_out = dot_nn(ot[...], cot_ref[...]).astype(BF16)
    grad_out_ref[...] = grad_out
    at = pl.program_id(0)
    rows = D // count
    split = grads_ref.shape[2]
    cols = pl.ds(pl.multiple_of(at * 3 * PAIR, PAIR), 3 * PAIR)
    for owner in range(count):
        own = grad_w[owner * rows : (owner + 1) * rows, :]
        grads_ref[0, owner, :, cols] = own[:split]
        grads_ref[1, owner, : rows - split, cols] = own[split:]
    if 2 * split > rows:
        cols = pl.ds(pl.multiple_of(lax.rem(at, each) * D, D), D)
        grads_ref[1, at // each, rows - split :, cols] = grad_out


def attention(low, low_t, cot, both, mix_bias, tables, start, first, each, shared, waits):
    length = low.shape[0]
    count = lax.axis_size("shard")
    first_block = start[0, ::BLK] // BLK
    rows = D // count
    joint = count == 2

    def pair(at):
        return at // each * (PAIRS // 2) + first + at % each

    def weight(offset):
        return pl.BlockSpec((D, PAIR), lambda at, _: (0, offset + pair(at)))

    def bias(offset):
        return pl.BlockSpec((1, PAIR), lambda at, _: (0, offset + pair(at)))

    def fixed(*shape):
        return pl.BlockSpec(shape, lambda at, _: (0,) * len(shape))

    pairs = 2 * each
    grads = (2, count, (rows + (PAIR if joint else 0)) // 2, pairs * 3 * PAIR)
    return pl.pallas_call(
        lambda *refs: attention_kernel(*refs, each=each, count=count),
        grid_spec=pltpu.PrefetchScalarGridSpec(
            num_scalar_prefetch=1,
            grid=(pairs,),
            in_specs=[
                fixed(length, D), fixed(D, length), fixed(length, D),
                weight(0), weight(PAIRS), weight(2 * PAIRS),
                bias(0), bias(PAIRS), bias(2 * PAIRS),
                pl.BlockSpec((PAIR, D), lambda at, _: (pair(at), 3)),
                fixed(length, PAIR), fixed(length, PAIR), fixed(length, PAIR), fixed(1, length),
            ]
            + [pl.BlockSpec(memory_space=pl.ANY)] * len((*shared, *waits)),
            out_specs=[
                pl.BlockSpec((length, PAIR), lambda at, _: (0, pair(at))),
                pl.BlockSpec((3, length, PAIR), lambda at, _: (0, 0, pair(at))),
                fixed(*grads),
                pl.BlockSpec((PAIR, D), lambda at, _: (at, 0)),
                pl.BlockSpec((1, 3 * PAIR), lambda at, _: (0, pair(at))),
            ],
            scratch_shapes=[pltpu.VMEM((length, PAIR), BF16)] * 3
            + [pltpu.VMEM((PAIR, length), BF16)] * 2
            + [pltpu.VMEM((length, PAIR), F32)] * 2
            + [
                pltpu.VMEM((length, PAIR), BF16), pltpu.VMEM((PAIR, length), BF16),
                pltpu.VMEM((D, 3 * PAIR), BF16),
            ],
        ),
        out_shape=[
            jax.ShapeDtypeStruct((length, D), BF16),
            jax.ShapeDtypeStruct((3, length, D), BF16),
            jax.ShapeDtypeStruct(grads, BF16),
            jax.ShapeDtypeStruct((pairs * PAIR, D), BF16),
            jax.ShapeDtypeStruct((1, 3 * D), F32),
        ],
        compiler_params=pltpu.CompilerParams(vmem_limit_bytes=VMEM_LIMIT),
        cost_estimate=pl.CostEstimate(
            flops=pairs * (20 * length * D * PAIR + 12 * length * 640 * HEAD_DIM * 16),
            bytes_accessed=6 * length * D + pairs * (D * PAIR * 16 + length * PAIR * 8),
            transcendentals=pairs * 2 * length * 640,
        ),
        input_output_aliases=dict(zip((15, 16, 17), (0, 1, 4))) if shared else {},
        name="attention",
    )(
        first_block, low, low_t, cot, both, both, both, mix_bias, mix_bias, mix_bias, both, *tables,
        start, *shared, *waits,
    )


def errors_kernel(
    grad_ref, rise_ref, back_ref, both_ref, tokens_ref, cot_ref, gain_one_ref, gain_two_ref, *rest,
):
    out_ref, sums_ref = rest[-2:]
    inputs = tokens_ref[...].astype(F32)
    upstream = cot_ref[...].astype(F32)
    center = inputs - jnp.mean(inputs, axis=-1, keepdims=True)
    inverse = lax.rsqrt(jnp.mean(center * center, axis=-1, keepdims=True) + EPS)
    unit = center * inverse
    error_two = dot_nt(grad_ref[...], rise_ref[...])
    error_one = dot_nt(back_ref[0], both_ref[:, :D])
    error_one += dot_nt(back_ref[1], both_ref[:, D : 2 * D])
    error_one += dot_nt(back_ref[2], both_ref[:, 2 * D :])
    total = upstream
    for error, gain_ref in ((error_one, gain_one_ref), (error_two, gain_two_ref)):
        scaled = error * gain_ref[...]
        total += inverse * (
            scaled
            - jnp.mean(scaled, axis=-1, keepdims=True)
            - unit * jnp.mean(scaled * unit, axis=-1, keepdims=True)
        )
    out_ref[...] = total
    sums = [error_one * unit, error_one, error_two * unit, error_two, upstream]

    @pl.when(pl.program_id(0) == 0)
    def _():
        sums_ref[...] = jnp.zeros_like(sums_ref)

    for row, value in enumerate(sums):
        sums_ref[row : row + 1, :] += jnp.sum(value, axis=0, keepdims=True)


def input_errors(grad, rise, back, both, tokens, cot, gain_one, gain_two, waits):
    length, hidden = grad.shape

    def rows(wide):
        return pl.BlockSpec((BLK, wide), lambda at: (at, 0))

    def fixed(*shape):
        return pl.BlockSpec(shape, lambda at: (0,) * len(shape))

    return pl.pallas_call(
        errors_kernel,
        grid=(length // BLK,),
        in_specs=[
            rows(hidden), fixed(D, hidden), pl.BlockSpec((3, BLK, D), lambda at: (0, at, 0)),
            fixed(D, 3 * D), rows(D), rows(D), fixed(1, D), fixed(1, D),
        ]
        + [pl.BlockSpec(memory_space=pl.ANY)] * len(waits),
        out_specs=[rows(D), fixed(8, D)],
        out_shape=[jax.ShapeDtypeStruct((length, D), F32), jax.ShapeDtypeStruct((8, D), F32)],
        compiler_params=pltpu.CompilerParams(vmem_limit_bytes=VMEM_LIMIT),
        cost_estimate=pl.CostEstimate(flops=1000, bytes_accessed=1000, transcendentals=0),
        name="input_errors",
    )(grad, rise, back, both, tokens, cot, gain_one, gain_two, *waits)


def output_kernel(act_ref, fall_ref, heads_ref, out_w_ref, tokens_ref, bias_ref, *rest):
    branches = dot_nn(act_ref[...], fall_ref[...]) + dot_nn(heads_ref[...], out_w_ref[...])
    total = tokens_ref[...].astype(F32) + branches + bias_ref[...]
    rest[-2][...] = total.astype(BF16)
    rest[-1][...] = total[:1, :PAIR]


def block_output(act, fall, heads, both, tokens, bias, waits):
    length, hidden = act.shape

    def rows(wide):
        return pl.BlockSpec((BLK, wide), lambda at: (at, 0))

    return pl.pallas_call(
        output_kernel,
        grid=(length // BLK,),
        in_specs=[
            rows(hidden), pl.BlockSpec((hidden, D), lambda at: (0, 0)), rows(D),
            pl.BlockSpec((D, D), lambda at: (0, 3)), rows(D), pl.BlockSpec((1, D), lambda at: (0, 0)),
        ]
        + [pl.BlockSpec(memory_space=pl.ANY)] * len(waits),
        out_specs=[rows(D), pl.BlockSpec((1, PAIR), lambda at: (0, 0))],
        out_shape=[
            jax.ShapeDtypeStruct((length, D), BF16), jax.ShapeDtypeStruct((1, PAIR), F32),
        ],
        compiler_params=pltpu.CompilerParams(vmem_limit_bytes=VMEM_LIMIT),
        cost_estimate=pl.CostEstimate(flops=1000, bytes_accessed=1000, transcendentals=0),
        name="block_output",
    )(act, fall, heads, both, tokens, bias, *waits)


def rotary_tables(segments):
    length = segments.shape[1]
    half = ROT // 2
    position = jnp.arange(length, dtype=jnp.int32)[None]
    change = jnp.concatenate(
        [jnp.ones((1, 1), dtype=bool), segments[:, 1:] != segments[:, :-1]], axis=1
    )
    start = lax.cummax(jnp.where(change, position, 0), axis=1)
    place = (position - start).astype(F32)
    frequency = 10000.0 ** (-2.0 * jnp.arange(half, dtype=F32) / ROT)
    angles = place[0][:, None] * frequency
    cosine, sine = jnp.cos(angles), jnp.sin(angles)
    rest = HEAD_DIM - ROT
    zero = jnp.zeros((length, half), F32)
    zeros = jnp.zeros((length, rest), F32)
    tables = (
        jnp.concatenate([cosine, cosine, jnp.ones((length, rest), F32)], axis=1),
        jnp.concatenate([-sine, zero, zeros], axis=1),
        jnp.concatenate([zero, sine, zeros], axis=1),
    )
    return start, [jnp.tile(table, (1, 2)) for table in tables]


def tie(value, *others):
    return lax.optimization_barrier((value, *others))[0]


def bit_of(axis, mask):
    return (lax.axis_index(axis) // mask) % 2


def swap(value, axis, mask):
    size = lax.axis_size(axis)
    return lax.ppermute(value, axis, [(i, i ^ mask) for i in range(size)])


def log2(size):
    return size.bit_length() - 1


class Chain:
    def __init__(self, steps):
        self.steps = steps
        self.result = None
        self.last = None

    def step(self, *after):
        if self.result is not None:
            return self.last
        try:
            self.last = next(self.steps) if self.last is None else self.steps.send(after)
        except StopIteration as stop:
            self.result = self.last = stop.value
        return self.last

    def finish(self, *after):
        while self.result is None:
            self.step(*after)
        return self.result


def arrived(value, after):
    return tie(value, *after) if after else value


def joined(mine, other, bit):
    return jnp.where(bit == 1, jnp.stack([other, mine]), jnp.stack([mine, other]))


def own_part(weight):
    parts = lax.axis_size("x") * lax.axis_size("c")
    rows = weight.shape[0] // parts
    at = lax.axis_index(("x", "c")) * rows
    return lax.dynamic_slice_in_dim(weight, at, rows, axis=0)


def gather_rows(weight):
    return lax.all_gather(own_part(weight), ("shard", "x", "c"), axis=0, tiled=True)


def gather_steps(weight, *after):
    other = own_part(weight)
    other = tie(other, *after) if after else other
    got = swap(other, "shard", 1)
    other = arrived(got, (yield other))
    for axis, at in (("x", 0), ("c", 1)):
        got = swap(other, axis, 1)
        got = arrived(got, (yield other))
        bit = lax.axis_index(axis)
        other = jnp.where(
            bit == 1, jnp.stack([got, other], at), jnp.stack([other, got], at)
        )
    other = other.reshape(weight.shape)
    return joined(weight, other, lax.axis_index("shard")).reshape(-1, weight.shape[1])


def sum_steps(grads, late=()):
    dims = [("c", 1)]
    dims += [("shard", 1 << i) for i in reversed(range(log2(lax.axis_size("shard"))))]
    rep = [("x", 1)] + [("z", 1 << i) for i in range(log2(lax.axis_size("z")))]
    parts = grads
    for dim in dims + rep:
        half = parts.reshape(2, -1, grads.shape[-1])
        bit = bit_of(*dim)
        send = lax.dynamic_index_in_dim(half, 1 - bit, axis=0, keepdims=False)
        got = swap(send, *dim)
        got = arrived(got, (yield send))
        keep = lax.dynamic_index_in_dim(half, bit, axis=0, keepdims=False)
        parts = (keep.astype(F32) + got.astype(F32)).astype(BF16)
    for dim in rep[::-1] + dims[:1]:
        got = swap(parts, *dim)
        after = yield parts
        got = arrived(got, (*after, *(late if dim == dims[0] else ())))
        parts = joined(parts, got, bit_of(*dim)).reshape(-1, grads.shape[-1])
    return parts.reshape(2, -1, grads.shape[-1])


def sum_offloaded(grads):
    parts = grads.reshape(-1, grads.shape[-1])
    parts = lax.psum_scatter(parts, ("shard", "c", "x"), scatter_dimension=0, tiled=True)
    yield parts
    parts = lax.psum_scatter(parts, "z", scatter_dimension=0, tiled=True)
    yield parts
    parts = lax.all_gather(parts, ("c", "x", "z"), axis=0, tiled=True)
    return parts.reshape(grads.shape[1:])


def total_steps(totals):
    rep = [("c", 1), ("x", 1)] + [("z", 1 << i) for i in range(log2(lax.axis_size("z")))]
    parts = totals
    for mask in [1 << i for i in reversed(range(log2(totals.shape[0])))]:
        half = parts.reshape(2, -1)
        bit = bit_of("shard", mask)
        send = lax.dynamic_index_in_dim(half, 1 - bit, axis=0, keepdims=False).astype(BF16)
        got = swap(send, "shard", mask)
        got = arrived(got, (yield send))
        parts = lax.dynamic_index_in_dim(half, bit, axis=0, keepdims=False) + got.astype(F32)
    for dim in rep:
        sent = parts.reshape(-1).astype(BF16)
        got = swap(sent, *dim)
        got = arrived(got, (yield sent))
        parts = sent.astype(F32) + got.astype(F32)
    return parts


def shards(
    tokens, segments, attn_gain, attn_shift, qkv_weight, qkv_bias, proj_weight, proj_bias,
    mlp_gain, mlp_shift, up_weight, up_bias, down_weight, down_bias, cotangent,
):
    count = lax.axis_size("shard")
    joint = count == 2
    small = [attn_gain, attn_shift, qkv_bias, proj_bias, mlp_gain, mlp_shift, up_bias, down_bias]
    sizes = [vector.shape[0] for vector in small]
    edges = [sum(sizes[:i]) for i in range(len(sizes) + 1)]
    own_small = jnp.concatenate(small)[None]
    own_both = jnp.concatenate([qkv_weight, proj_weight], axis=1)
    if joint:
        small_all = joined(own_small, swap(own_small, "shard", 1), lax.axis_index("shard"))
        small_all = small_all.reshape(2, -1)
        rise_chain, fall_chain, both_chain = [
            Chain(gather_steps(weight)) for weight in (up_weight, down_weight, own_both)
        ]
        rise_chain.step()
        mark = rise_chain.step()
        fall_chain.steps = gather_steps(down_weight, mark)
        fall_chain.step()
        rise_chain.step()
        mark = fall_chain.step()
        both_chain.steps = gather_steps(own_both, mark)
        both_chain.step()
        rise = rise_chain.finish()
        mark = fall_chain.step()
        both_chain.step(mark)
        fall = fall_chain.finish()
    else:
        small_all = lax.all_gather(own_small, "shard", axis=0, tiled=True)
        rise, fall, both = [gather_rows(w) for w in (up_weight, down_weight, own_both)]
    gain_one, shift_one, mix_bias, out_bias, gain_two, shift_two, rise_bias, fall_bias = [
        small_all[:, a:b].reshape(1, -1).astype(F32) for a, b in zip(edges[:-1], edges[1:])
    ]

    inputs = tokens.astype(F32)
    start, tables = rotary_tables(segments)
    center = inputs - jnp.mean(inputs, axis=-1, keepdims=True)
    inverse = lax.rsqrt(jnp.mean(center * center, axis=-1, keepdims=True) + EPS)
    unit = center * inverse
    low_one = (unit * gain_one + shift_one).astype(BF16)
    low_two = (unit * gain_two + shift_two).astype(BF16)
    low_one_t = low_one.T
    low_two_t = low_two.T
    rows = D // count
    each = (2, 1)
    waits = (both_chain.last,) if joint else ()
    act, act_back, mlp_grads, rise_total = mlp(
        low_two, low_two_t, cotangent, rise, rise_bias, fall, waits
    )
    mlp_chain = Chain(sum_offloaded(mlp_grads))
    scattered = mlp_chain.step()
    if joint:
        both_chain.step(rise_total)
        both = both_chain.finish()

    def attend(first, each, shared, *waits):
        return attention(
            low_one, low_one_t, cotangent, both, mix_bias, tables, start, first, each, shared, waits
        )

    out_a, back_a, grads_a, grad_out_a, total_a = attend(0, each[0], (), rise_total)
    late = []
    sum_a = Chain(sum_steps(grads_a, late))
    sum_a.step()
    sent = sum_a.step()
    heads, back, grads_b, grad_out_b, mix_total = attend(
        each[0], each[1], (out_a, back_a, total_a), sent, scattered
    )
    sum_b = Chain(sum_steps(grads_b, late))
    marks = [mlp_chain.step(), sum_b.step(), sum_a.step(mix_total)]
    tokens_grad, sums = input_errors(
        act_back, rise, back, both, tokens, cotangent, gain_one, gain_two, marks
    )
    mlp_own = mlp_chain.finish()
    late.append(mlp_own[0, :1, :PAIR])
    mix_total = mix_total.reshape(PAIRS, 3, PAIR).swapaxes(0, 1)
    totals = [sums[:5].reshape(5, count, rows).swapaxes(0, 1), mix_total, rise_total]
    totals = jnp.concatenate([t.reshape(count, -1) for t in totals], axis=1)
    total_chain = Chain(total_steps(totals))
    marks = [total_chain.step(), sum_b.step(sums), sum_a.step(sums)]
    result, mark = block_output(act, fall, heads, both, tokens, out_bias + fall_bias, marks)
    for chain in (total_chain, sum_b, sum_a):
        chain.step(mark)
    owned = total_chain.finish()
    mix_own = [sum_a.finish(), sum_b.finish()]
    vectors = owned[: 5 * rows].reshape(5, rows)
    mix_vector, rise_vector = owned[5 * rows : 8 * rows], owned[8 * rows :]

    sum_fall = mlp_own[0].astype(F32)
    blocks = mlp_own[1].reshape(-1, rows, D)
    sum_rise = jnp.concatenate(list(blocks), axis=1).astype(F32)
    mix_own = [own.reshape(-1, own.shape[-1]) for own in mix_own]
    pair_rows = [own[:rows].reshape(rows, 2, n, 3, PAIR) for own, n in zip(mix_own, each)]
    sum_mix = jnp.concatenate(
        [
            part[:, half, at, kind]
            for kind in range(3)
            for half in range(2)
            for part, n in zip(pair_rows, each)
            for at in range(n)
        ],
        axis=1,
    ).astype(F32)
    if joint:
        blocks = [
            own[rows:, at * D : (at + 1) * D] for own, n in zip(mix_own, each) for at in range(n)
        ]
        sum_out = jnp.concatenate(blocks, axis=0).astype(F32)
    else:
        grads = [g.reshape(2, -1, D) for g in (grad_out_a, grad_out_b)]
        grads = jnp.concatenate(grads, axis=1).reshape(count, 2, rows // 2, D).swapaxes(0, 1)
        sum_out = Chain(sum_steps(grads)).finish().reshape(rows, D).astype(F32)
    return (
        result, tokens_grad, vectors[0], vectors[1], sum_mix, mix_vector, sum_out, vectors[4],
        vectors[2], vectors[3], sum_rise, rise_vector, sum_fall, vectors[4],
    )


def solution(mesh):
    reps, count = mesh.devices.shape
    fine = Mesh(mesh.devices.reshape(reps // 4, 2, 2, count), (*REP, "shard"))
    rows = P((*REP, "shard"), None)
    line = P("shard")
    wide = P("shard", None)
    in_specs = (
        rows, rows, line, line, wide, line, wide, line, line, line, wide, line, wide, line, rows,
    )
    out_specs = (
        rows, rows, line, line, wide, line, wide, line, line, line, wide, line, wide, line,
    )
    return jax.shard_map(shards, mesh=fine, in_specs=in_specs, out_specs=out_specs, check_vma=False)
```

```python
import math

import jax
import jax.numpy as jnp
from jax import lax
from jax.experimental import pallas as pl
from jax.experimental.pallas import tpu as pltpu
from jax.sharding import Mesh
from jax.sharding import PartitionSpec as P

D = 768
HEADS = 12
HEAD_DIM = 64
ROT = 16
BLK = 256
PAIR = 2 * HEAD_DIM
PAIRS = HEADS // 2
SPAN = 3
EPS = 1e-05
F32 = jnp.float32
BF16 = jnp.bfloat16
REP = ("z", "x", "c")
VMEM_LIMIT = 56 * 1024 * 1024


def dot_nt(left, right):
    return lax.dot_general(left, right, (((1,), (1,)), ((), ())), preferred_element_type=F32)


def dot_nn(left, right):
    return lax.dot_general(left, right, (((1,), (0,)), ((), ())), preferred_element_type=F32)


def dot_tn(left, right):
    return lax.dot_general(left, right, (((0,), (0,)), ((), ())), preferred_element_type=F32)


def mlp_kernel(
    low_ref, low_t_ref, cot_ref, rise_ref, bias_ref, fall_ref, *rest, per_shard, count,
):
    act_ref, back_ref, grads_ref, total_ref, slope = rest[-5:]
    at = pl.program_id(0)
    tile = rise_ref.shape[1]
    before = dot_nn(low_ref[...], rise_ref[...]) + bias_ref[...]
    chance = 0.5 + 0.5 * lax.erf(before * (1.0 / math.sqrt(2.0)))
    slope[...] = chance + before * jnp.exp(-0.5 * before * before) * (1.0 / math.sqrt(2.0 * math.pi))
    act_ref[...] = (before * chance).astype(BF16)
    grad_fall = dot_tn(act_ref[...], cot_ref[...]).astype(BF16)
    owner_fall = at // per_shard
    place = pl.ds(pl.multiple_of(lax.rem(at, per_shard) * tile, tile), tile)
    grads_ref[owner_fall, 0, place, :] = grad_fall
    back_ref[...] = (dot_nt(cot_ref[...], fall_ref[...]) * slope[...]).astype(BF16)
    low_grad = back_ref[...]
    total_ref[...] = jnp.sum(low_grad.astype(F32), axis=0, keepdims=True)
    grad_rise = dot_nn(low_t_ref[...], low_grad).astype(BF16)
    rows = D // count
    wide = D // tile
    block = at // wide
    cols = pl.ds(pl.multiple_of(lax.rem(at, wide) * tile, tile), tile)
    for owner in range(count):
        at_rows = pl.ds(pl.multiple_of(block * rows, rows), rows)
        grads_ref[owner, 1, at_rows, cols] = grad_rise[owner * rows : (owner + 1) * rows, :]


def mlp(low, low_t, cot, rise, bias, fall, waits):
    length = low.shape[0]
    hidden = rise.shape[1]
    count = lax.axis_size("shard")
    width = hidden // count
    tile = 256 if width % 256 == 0 else 128
    whole = pl.BlockSpec((length, D), lambda at: (0, 0))
    column = pl.BlockSpec((length, tile), lambda at: (0, at))
    line = pl.BlockSpec((1, tile), lambda at: (0, at))
    return pl.pallas_call(
        lambda *refs: mlp_kernel(*refs, per_shard=width // tile, count=count),
        grid=(hidden // tile,),
        in_specs=[
            whole,
            pl.BlockSpec((D, length), lambda at: (0, 0)),
            whole,
            pl.BlockSpec((D, tile), lambda at: (0, at)),
            line,
            pl.BlockSpec((tile, D), lambda at: (at, 0)),
        ]
        + [pl.BlockSpec(memory_space=pl.ANY)] * len(waits),
        out_specs=[
            column,
            column,
            pl.BlockSpec((count, 2, width, D), lambda at: (0, 0, 0, 0)),
            line,
        ],
        out_shape=[
            jax.ShapeDtypeStruct((length, hidden), BF16),
            jax.ShapeDtypeStruct((length, hidden), BF16),
            jax.ShapeDtypeStruct((count, 2, width, D), BF16),
            jax.ShapeDtypeStruct((1, hidden), F32),
        ],
        scratch_shapes=[pltpu.VMEM((length, tile), F32)],
        compiler_params=pltpu.CompilerParams(vmem_limit_bytes=VMEM_LIMIT),
        cost_estimate=pl.CostEstimate(
            flops=8 * length * D * hidden,
            bytes_accessed=6 * length * D + 8 * D * hidden + 4 * length * hidden,
            transcendentals=2 * length * hidden,
        ),
        name="mlp",
    )(low, low_t, cot, rise, bias, fall, *waits)


def attention_kernel(
    first_ref, low_ref, low_t_ref, cot_ref, wq_ref, wk_ref, wv_ref, bq_ref, bk_ref, bv_ref, out_w_ref,
    cos_ref, up_ref, down_ref, start_ref, *rest, each, count,
):
    (
        ob, back, grads_ref, grad_out_ref, total_ref, qs, ks, vs, kt, vt, dk, dv, gs, ot, w3,
    ) = rest[-15:]
    length = low_ref.shape[0]
    half = ROT // 2
    scale = HEAD_DIM ** -0.5

    def turn(x):
        return (
            x * cos_ref[...]
            + pltpu.roll(x, PAIR - half, 1) * up_ref[...]
            + pltpu.roll(x, half, 1) * down_ref[...]
        )

    def turn_back(g, rows):
        return (
            g * cos_ref[rows, :]
            + pltpu.roll(g * up_ref[rows, :], half, 1)
            + pltpu.roll(g * down_ref[rows, :], PAIR - half, 1)
        )

    w3[:, :PAIR] = wq_ref[...]
    w3[:, PAIR : 2 * PAIR] = wk_ref[...]
    w3[:, 2 * PAIR :] = wv_ref[...]
    mixed = dot_nn(low_ref[...], w3[...])
    qs[...] = turn(mixed[:, :PAIR] + bq_ref[...]).astype(BF16)
    keys = turn(mixed[:, PAIR : 2 * PAIR] + bk_ref[...]).astype(BF16)
    ks[...] = keys
    kt[...] = keys.astype(F32).T.astype(BF16)
    values = (mixed[:, 2 * PAIR :] + bv_ref[...]).astype(BF16)
    vs[...] = values
    vt[...] = values.astype(F32).T.astype(BF16)
    gs[...] = dot_nt(cot_ref[...], out_w_ref[...]).astype(BF16)
    dk[...] = jnp.zeros_like(dk)
    dv[...] = jnp.zeros_like(dv)
    low = lax.broadcasted_iota(jnp.int32, (BLK, PAIR), 1) < HEAD_DIM

    def block(at, blocks):
        extent = blocks * BLK
        query_at = pl.multiple_of(at * BLK, BLK)
        key_at = pl.multiple_of((at - blocks + 1) * BLK, BLK)
        rows = pl.ds(query_at, BLK)
        cols = pl.ds(key_at, extent)
        qb = qs[rows, :]
        gb = gs[rows, :]
        kb = ks[cols, :]
        vb = vs[cols, :]
        start = start_ref[:, rows]
        key_index = lax.broadcasted_iota(jnp.int32, (extent, BLK), 0)
        query_index = lax.broadcasted_iota(jnp.int32, (extent, BLK), 1) + (blocks - 1) * BLK
        allowed = (key_index >= start - key_at) & (key_index <= query_index)
        outs, dqs = [], []
        dk_new = dv_new = None
        for head in range(2):
            lanes = low if head == 0 else ~low
            part = slice(head * HEAD_DIM, (head + 1) * HEAD_DIM)
            qh = jnp.where(lanes, qb, jnp.zeros_like(qb))
            gh = jnp.where(lanes, gb, jnp.zeros_like(gb))
            scores = jnp.where(allowed, dot_nt(kb, qh) * (scale * math.log2(math.e)), -1e30)
            weight = jnp.exp2(scores - jnp.max(scores, axis=0, keepdims=True))
            probs = weight * (1.0 / jnp.sum(weight, axis=0, keepdims=True))
            low_probs = probs.astype(BF16)
            outs.append(dot_nn(vt[part, cols], low_probs))
            grad_probs = dot_nt(vb, gh)
            delta = jnp.sum(probs * grad_probs, axis=0, keepdims=True)
            grad_scores = (probs * (grad_probs - delta)).astype(BF16)
            dqs.append(dot_nn(kt[part, cols], grad_scores))
            dv_part = dot_nn(low_probs, gh)
            dk_part = dot_nn(grad_scores, qh)
            dv_new = dv_part if dv_new is None else dv_new + dv_part
            dk_new = dk_part if dk_new is None else dk_new + dk_part
        dv[cols, :] += dv_new
        dk[cols, :] += dk_new
        out_t = jnp.concatenate(outs, 0)
        ot[:, rows] = out_t.astype(BF16)
        ob[rows, :] = out_t.T.astype(BF16)
        back[0, rows, :] = turn_back(jnp.concatenate(dqs, 0).T * scale, rows).astype(BF16)

    def step(at, carry):
        needed = at - first_ref[at] + 1
        for blocks in range(1, SPAN + 1):
            pl.when(needed == blocks)(lambda blocks=blocks: block(at, blocks))
        return carry

    lax.fori_loop(0, length // BLK, step, 0)
    back[1] = turn_back(dk[...] * scale, slice(None)).astype(BF16)
    back[2] = dv[...].astype(BF16)
    grad_mixed = jnp.concatenate([back[0], back[1], back[2]], axis=1)
    total_ref[...] = jnp.sum(grad_mixed.astype(F32), axis=0, keepdims=True)
    grad_w = dot_nn(low_t_ref[...], grad_mixed).astype(BF16)
    grad_out = dot_nn(ot[...], cot_ref[...]).astype(BF16)
    grad_out_ref[...] = grad_out
    at = pl.program_id(0)
    rows = D // count
    split = grads_ref.shape[2]
    cols = pl.ds(pl.multiple_of(at * 3 * PAIR, PAIR), 3 * PAIR)
    for owner in range(count):
        own = grad_w[owner * rows : (owner + 1) * rows, :]
        grads_ref[0, owner, :, cols] = own[:split]
        grads_ref[1, owner, : rows - split, cols] = own[split:]
    if 2 * split > rows:
        cols = pl.ds(pl.multiple_of(lax.rem(at, each) * D, D), D)
        grads_ref[1, at // each, rows - split :, cols] = grad_out


def attention(low, low_t, cot, both, mix_bias, tables, start, first, each, shared, waits):
    length = low.shape[0]
    count = lax.axis_size("shard")
    first_block = start[0, ::BLK] // BLK
    rows = D // count
    joint = count == 2

    def pair(at):
        return at // each * (PAIRS // 2) + first + at % each

    def weight(offset):
        return pl.BlockSpec((D, PAIR), lambda at, _: (0, offset + pair(at)))

    def bias(offset):
        return pl.BlockSpec((1, PAIR), lambda at, _: (0, offset + pair(at)))

    def fixed(*shape):
        return pl.BlockSpec(shape, lambda at, _: (0,) * len(shape))

    pairs = 2 * each
    grads = (2, count, (rows + (PAIR if joint else 0)) // 2, pairs * 3 * PAIR)
    return pl.pallas_call(
        lambda *refs: attention_kernel(*refs, each=each, count=count),
        grid_spec=pltpu.PrefetchScalarGridSpec(
            num_scalar_prefetch=1,
            grid=(pairs,),
            in_specs=[
                fixed(length, D), fixed(D, length), fixed(length, D),
                weight(0), weight(PAIRS), weight(2 * PAIRS),
                bias(0), bias(PAIRS), bias(2 * PAIRS),
                pl.BlockSpec((PAIR, D), lambda at, _: (pair(at), 3)),
                fixed(length, PAIR), fixed(length, PAIR), fixed(length, PAIR), fixed(1, length),
            ]
            + [pl.BlockSpec(memory_space=pl.ANY)] * len((*shared, *waits)),
            out_specs=[
                pl.BlockSpec((length, PAIR), lambda at, _: (0, pair(at))),
                pl.BlockSpec((3, length, PAIR), lambda at, _: (0, 0, pair(at))),
                fixed(*grads),
                pl.BlockSpec((PAIR, D), lambda at, _: (at, 0)),
                pl.BlockSpec((1, 3 * PAIR), lambda at, _: (0, pair(at))),
            ],
            scratch_shapes=[pltpu.VMEM((length, PAIR), BF16)] * 3
            + [pltpu.VMEM((PAIR, length), BF16)] * 2
            + [pltpu.VMEM((length, PAIR), F32)] * 2
            + [
                pltpu.VMEM((length, PAIR), BF16), pltpu.VMEM((PAIR, length), BF16),
                pltpu.VMEM((D, 3 * PAIR), BF16),
            ],
        ),
        out_shape=[
            jax.ShapeDtypeStruct((length, D), BF16),
            jax.ShapeDtypeStruct((3, length, D), BF16),
            jax.ShapeDtypeStruct(grads, BF16),
            jax.ShapeDtypeStruct((pairs * PAIR, D), BF16),
            jax.ShapeDtypeStruct((1, 3 * D), F32),
        ],
        compiler_params=pltpu.CompilerParams(vmem_limit_bytes=VMEM_LIMIT),
        cost_estimate=pl.CostEstimate(flops=1000, bytes_accessed=1000, transcendentals=0),
        input_output_aliases=dict(zip((15, 16, 17), (0, 1, 4))) if shared else {},
        name="attention",
    )(
        first_block, low, low_t, cot, both, both, both, mix_bias, mix_bias, mix_bias, both, *tables,
        start, *shared, *waits,
    )


def errors_kernel(
    grad_ref, rise_ref, back_ref, both_ref, tokens_ref, cot_ref, gain_one_ref, gain_two_ref, *rest,
):
    out_ref, sums_ref = rest[-2:]
    inputs = tokens_ref[...].astype(F32)
    upstream = cot_ref[...].astype(F32)
    center = inputs - jnp.mean(inputs, axis=-1, keepdims=True)
    inverse = lax.rsqrt(jnp.mean(center * center, axis=-1, keepdims=True) + EPS)
    unit = center * inverse
    error_two = dot_nt(grad_ref[...], rise_ref[...])
    error_one = dot_nt(back_ref[0], both_ref[:, :D])
    error_one += dot_nt(back_ref[1], both_ref[:, D : 2 * D])
    error_one += dot_nt(back_ref[2], both_ref[:, 2 * D :])
    total = upstream
    for error, gain_ref in ((error_one, gain_one_ref), (error_two, gain_two_ref)):
        scaled = error * gain_ref[...]
        total += inverse * (
            scaled
            - jnp.mean(scaled, axis=-1, keepdims=True)
            - unit * jnp.mean(scaled * unit, axis=-1, keepdims=True)
        )
    out_ref[...] = total
    sums = [error_one * unit, error_one, error_two * unit, error_two, upstream]

    @pl.when(pl.program_id(0) == 0)
    def _():
        sums_ref[...] = jnp.zeros_like(sums_ref)

    for row, value in enumerate(sums):
        sums_ref[row : row + 1, :] += jnp.sum(value, axis=0, keepdims=True)


def input_errors(grad, rise, back, both, tokens, cot, gain_one, gain_two, waits):
    length, hidden = grad.shape

    def rows(wide):
        return pl.BlockSpec((BLK, wide), lambda at: (at, 0))

    def fixed(*shape):
        return pl.BlockSpec(shape, lambda at: (0,) * len(shape))

    return pl.pallas_call(
        errors_kernel,
        grid=(length // BLK,),
        in_specs=[
            rows(hidden), fixed(D, hidden), pl.BlockSpec((3, BLK, D), lambda at: (0, at, 0)),
            fixed(D, 3 * D), rows(D), rows(D), fixed(1, D), fixed(1, D),
        ]
        + [pl.BlockSpec(memory_space=pl.ANY)] * len(waits),
        out_specs=[rows(D), fixed(8, D)],
        out_shape=[jax.ShapeDtypeStruct((length, D), F32), jax.ShapeDtypeStruct((8, D), F32)],
        compiler_params=pltpu.CompilerParams(vmem_limit_bytes=VMEM_LIMIT),
        cost_estimate=pl.CostEstimate(flops=1000, bytes_accessed=1000, transcendentals=0),
        name="input_errors",
    )(grad, rise, back, both, tokens, cot, gain_one, gain_two, *waits)


def output_kernel(act_ref, fall_ref, heads_ref, out_w_ref, tokens_ref, bias_ref, *rest):
    branches = dot_nn(act_ref[...], fall_ref[...]) + dot_nn(heads_ref[...], out_w_ref[...])
    total = tokens_ref[...].astype(F32) + branches + bias_ref[...]
    rest[-2][...] = total.astype(BF16)
    rest[-1][...] = total[:1, :PAIR]


def block_output(act, fall, heads, both, tokens, bias, waits):
    length, hidden = act.shape

    def rows(wide):
        return pl.BlockSpec((BLK, wide), lambda at: (at, 0))

    return pl.pallas_call(
        output_kernel,
        grid=(length // BLK,),
        in_specs=[
            rows(hidden), pl.BlockSpec((hidden, D), lambda at: (0, 0)), rows(D),
            pl.BlockSpec((D, D), lambda at: (0, 3)), rows(D), pl.BlockSpec((1, D), lambda at: (0, 0)),
        ]
        + [pl.BlockSpec(memory_space=pl.ANY)] * len(waits),
        out_specs=[rows(D), pl.BlockSpec((1, PAIR), lambda at: (0, 0))],
        out_shape=[
            jax.ShapeDtypeStruct((length, D), BF16), jax.ShapeDtypeStruct((1, PAIR), F32),
        ],
        compiler_params=pltpu.CompilerParams(vmem_limit_bytes=VMEM_LIMIT),
        cost_estimate=pl.CostEstimate(flops=1000, bytes_accessed=1000, transcendentals=0),
        name="block_output",
    )(act, fall, heads, both, tokens, bias, *waits)


def widen_mlp_kernel(fall_ref, rise_ref, fall_out, rise_out, mark_ref):
    fall_out[...] = fall_ref[0].astype(F32)
    rise_out[...] = rise_ref[0].astype(F32)
    mark_ref[...] = fall_out[:1, :PAIR]


def widen_mlp(owned):
    _, width, _ = owned.shape
    rows = D // lax.axis_size("shard")
    return pl.pallas_call(
        widen_mlp_kernel,
        grid=(width // rows,),
        in_specs=[pl.BlockSpec((1, rows, D), lambda at, kind=kind: (kind, at, 0)) for kind in (0, 1)],
        out_specs=[
            pl.BlockSpec((rows, D), lambda at: (at, 0)),
            pl.BlockSpec((rows, D), lambda at: (0, at)),
            pl.BlockSpec((1, PAIR), lambda at: (0, 0)),
        ],
        out_shape=[
            jax.ShapeDtypeStruct((width, D), F32),
            jax.ShapeDtypeStruct((rows, width // rows * D), F32),
            jax.ShapeDtypeStruct((1, PAIR), F32),
        ],
        name="widen_mlp",
    )(owned, owned)


def widen_mix_kernel(first_ref, second_ref, mix_out, out_out):
    rows = mix_out.shape[0]
    third = PAIRS // 2
    for pair in range(PAIRS):
        half, at = pair // third, pair % third
        ref, place = (first_ref, half * 2 + at) if at < 2 else (second_ref, half)
        for kind in range(3):
            to = (kind * PAIRS + pair) * PAIR
            source = (place * 3 + kind) * PAIR
            mix_out[:, to : to + PAIR] = ref[:rows, source : source + PAIR].astype(F32)
    for at in range(third):
        ref, source = (first_ref, at * D) if at < 2 else (second_ref, 0)
        out_out[at * PAIR : (at + 1) * PAIR, :] = ref[rows:, source : source + D].astype(F32)


def widen_mix(first, second):
    rows = D // lax.axis_size("shard")
    return pl.pallas_call(
        widen_mix_kernel,
        out_shape=[jax.ShapeDtypeStruct((rows, 3 * D), F32), jax.ShapeDtypeStruct((rows, D), F32)],
        compiler_params=pltpu.CompilerParams(vmem_limit_bytes=VMEM_LIMIT),
        name="widen_mix",
    )(first, second)


def rotary_tables(segments):
    length = segments.shape[1]
    half = ROT // 2
    position = jnp.arange(length, dtype=jnp.int32)[None]
    change = jnp.concatenate(
        [jnp.ones((1, 1), dtype=bool), segments[:, 1:] != segments[:, :-1]], axis=1
    )
    start = lax.cummax(jnp.where(change, position, 0), axis=1)
    place = (position - start).astype(F32)
    frequency = 10000.0 ** (-2.0 * jnp.arange(half, dtype=F32) / ROT)
    angles = place[0][:, None] * frequency
    cosine, sine = jnp.cos(angles), jnp.sin(angles)
    rest = HEAD_DIM - ROT
    zero = jnp.zeros((length, half), F32)
    zeros = jnp.zeros((length, rest), F32)
    tables = (
        jnp.concatenate([cosine, cosine, jnp.ones((length, rest), F32)], axis=1),
        jnp.concatenate([-sine, zero, zeros], axis=1),
        jnp.concatenate([zero, sine, zeros], axis=1),
    )
    return start, [jnp.tile(table, (1, 2)) for table in tables]


def tie(value, *others):
    return lax.optimization_barrier((value, *others))[0]


def bit_of(axis, mask):
    return (lax.axis_index(axis) // mask) % 2


def swap(value, axis, mask):
    size = lax.axis_size(axis)
    return lax.ppermute(value, axis, [(i, i ^ mask) for i in range(size)])


def log2(size):
    return size.bit_length() - 1


class Chain:
    def __init__(self, steps):
        self.steps = steps
        self.result = None
        self.last = None

    def step(self, *after):
        if self.result is not None:
            return self.last
        try:
            self.last = next(self.steps) if self.last is None else self.steps.send(after)
        except StopIteration as stop:
            self.result = self.last = stop.value
        return self.last

    def finish(self, *after):
        while self.result is None:
            self.step(*after)
        return self.result


def arrived(value, after):
    return tie(value, *after) if after else value


def joined(mine, other, bit):
    return jnp.where(bit == 1, jnp.stack([other, mine]), jnp.stack([mine, other]))


def own_part(weight):
    parts = lax.axis_size("x") * lax.axis_size("c")
    rows = weight.shape[0] // parts
    at = lax.axis_index(("x", "c")) * rows
    return lax.dynamic_slice_in_dim(weight, at, rows, axis=0)


def gather_rows(weight):
    return lax.all_gather(own_part(weight), ("shard", "x", "c"), axis=0, tiled=True)


def gather_steps(weight, *after):
    other = own_part(weight)
    other = tie(other, *after) if after else other
    got = swap(other, "shard", 1)
    other = arrived(got, (yield other))
    for axis, at in (("x", 0), ("c", 1)):
        got = swap(other, axis, 1)
        got = arrived(got, (yield other))
        bit = lax.axis_index(axis)
        other = jnp.where(
            bit == 1, jnp.stack([got, other], at), jnp.stack([other, got], at)
        )
    other = other.reshape(weight.shape)
    return joined(weight, other, lax.axis_index("shard")).reshape(-1, weight.shape[1])


def sum_steps(grads, late=()):
    dims = [("c", 1)]
    dims += [("shard", 1 << i) for i in reversed(range(log2(lax.axis_size("shard"))))]
    rep = [("x", 1)] + [("z", 1 << i) for i in range(log2(lax.axis_size("z")))]
    parts = grads
    for dim in dims + rep:
        half = parts.reshape(2, -1, grads.shape[-1])
        bit = bit_of(*dim)
        send = lax.dynamic_index_in_dim(half, 1 - bit, axis=0, keepdims=False)
        got = swap(send, *dim)
        got = arrived(got, (yield send))
        keep = lax.dynamic_index_in_dim(half, bit, axis=0, keepdims=False)
        parts = (keep.astype(F32) + got.astype(F32)).astype(BF16)
    for dim in rep[::-1] + dims[:1]:
        got = swap(parts, *dim)
        after = yield parts
        got = arrived(got, (*after, *(late if dim == dims[0] else ())))
        parts = joined(parts, got, bit_of(*dim)).reshape(-1, grads.shape[-1])
    return parts.reshape(2, -1, grads.shape[-1])


def sum_offloaded(grads):
    parts = grads.reshape(-1, grads.shape[-1])
    parts = lax.psum_scatter(parts, ("shard", "c", "x", "z"), scatter_dimension=0, tiled=True)
    parts = arrived(parts, (yield parts))
    yield parts
    parts = lax.all_gather(parts, ("c", "x", "z"), axis=0, tiled=True)
    return parts.reshape(grads.shape[1:])


def total_steps(totals):
    rep = [("c", 1), ("x", 1)] + [("z", 1 << i) for i in range(log2(lax.axis_size("z")))]
    parts = totals
    for mask in [1 << i for i in reversed(range(log2(totals.shape[0])))]:
        half = parts.reshape(2, -1)
        bit = bit_of("shard", mask)
        send = lax.dynamic_index_in_dim(half, 1 - bit, axis=0, keepdims=False).astype(BF16)
        got = swap(send, "shard", mask)
        got = arrived(got, (yield send))
        parts = lax.dynamic_index_in_dim(half, bit, axis=0, keepdims=False) + got.astype(F32)
    for dim in rep:
        sent = parts.reshape(-1).astype(BF16)
        got = swap(sent, *dim)
        got = arrived(got, (yield sent))
        parts = sent.astype(F32) + got.astype(F32)
    return parts


def shards(
    tokens, segments, attn_gain, attn_shift, qkv_weight, qkv_bias, proj_weight, proj_bias,
    mlp_gain, mlp_shift, up_weight, up_bias, down_weight, down_bias, cotangent,
):
    count = lax.axis_size("shard")
    joint = count == 2
    small = [attn_gain, attn_shift, qkv_bias, proj_bias, mlp_gain, mlp_shift, up_bias, down_bias]
    sizes = [vector.shape[0] for vector in small]
    edges = [sum(sizes[:i]) for i in range(len(sizes) + 1)]
    own_small = jnp.concatenate(small)[None]
    own_both = jnp.concatenate([qkv_weight, proj_weight], axis=1)
    if joint:
        small_all = joined(own_small, swap(own_small, "shard", 1), lax.axis_index("shard"))
        small_all = small_all.reshape(2, -1)
        rise_chain, fall_chain, both_chain = [
            Chain(gather_steps(weight)) for weight in (up_weight, down_weight, own_both)
        ]
        rise_chain.step()
        mark = rise_chain.step()
        fall_chain.steps = gather_steps(down_weight, mark)
        fall_chain.step()
        rise_chain.step()
        mark = fall_chain.step()
        both_chain.steps = gather_steps(own_both, mark)
        both_chain.step()
        rise = rise_chain.finish()
        mark = fall_chain.step()
        both_chain.step(mark)
        fall = fall_chain.finish()
    else:
        small_all = lax.all_gather(own_small, "shard", axis=0, tiled=True)
        rise, fall, both = [gather_rows(w) for w in (up_weight, down_weight, own_both)]
    gain_one, shift_one, mix_bias, out_bias, gain_two, shift_two, rise_bias, fall_bias = [
        small_all[:, a:b].reshape(1, -1).astype(F32) for a, b in zip(edges[:-1], edges[1:])
    ]

    inputs = tokens.astype(F32)
    start, tables = rotary_tables(segments)
    center = inputs - jnp.mean(inputs, axis=-1, keepdims=True)
    inverse = lax.rsqrt(jnp.mean(center * center, axis=-1, keepdims=True) + EPS)
    unit = center * inverse
    low_one = (unit * gain_one + shift_one).astype(BF16)
    low_two = (unit * gain_two + shift_two).astype(BF16)
    low_one_t = low_one.T
    low_two_t = low_two.T
    rows = D // count
    each = (2, 1)
    waits = (both_chain.last,) if joint else ()
    act, act_back, mlp_grads, rise_total = mlp(
        low_two, low_two_t, cotangent, rise, rise_bias, fall, waits
    )
    mlp_chain = Chain(sum_offloaded(mlp_grads))
    mlp_chain.step()
    if joint:
        both_chain.step(rise_total)
        both = both_chain.finish()

    def attend(first, each, shared, *waits):
        return attention(
            low_one, low_one_t, cotangent, both, mix_bias, tables, start, first, each, shared, waits
        )

    out_a, back_a, grads_a, grad_out_a, total_a = attend(0, each[0], (), rise_total)
    late = []
    sum_a = Chain(sum_steps(grads_a, late))
    sum_a.step()
    sent = sum_a.step()
    heads, back, grads_b, grad_out_b, mix_total = attend(
        each[0], each[1], (out_a, back_a, total_a), sent
    )
    sum_b = Chain(sum_steps(grads_b, late))
    sum_b.step()
    marks = [mlp_chain.step(mix_total), sum_a.step(mix_total), sum_b.step()]
    tokens_grad, sums = input_errors(
        act_back, rise, back, both, tokens, cotangent, gain_one, gain_two, marks
    )
    mlp_own = mlp_chain.finish()
    sum_fall, sum_rise, widened = widen_mlp(mlp_own)
    late.append(widened)
    mix_total = mix_total.reshape(PAIRS, 3, PAIR).swapaxes(0, 1)
    totals = [sums[:5].reshape(5, count, rows).swapaxes(0, 1), mix_total, rise_total]
    totals = jnp.concatenate([t.reshape(count, -1) for t in totals], axis=1)
    total_chain = Chain(total_steps(totals))
    marks = [total_chain.step(), sum_b.step(sums), sum_a.step(sums)]
    result, mark = block_output(act, fall, heads, both, tokens, out_bias + fall_bias, marks)
    for chain in (total_chain, sum_b, sum_a):
        chain.step(mark)
    owned = total_chain.finish()
    mix_own = [sum_a.finish(), sum_b.finish()]
    vectors = owned[: 5 * rows].reshape(5, rows)
    mix_vector, rise_vector = owned[5 * rows : 8 * rows], owned[8 * rows :]

    mix_own = [own.reshape(-1, own.shape[-1]) for own in mix_own]
    if joint:
        sum_mix, sum_out = widen_mix(*mix_own)
    else:
        pair_rows = [own[:rows].reshape(rows, 2, n, 3, PAIR) for own, n in zip(mix_own, each)]
        sum_mix = jnp.concatenate(
            [
                part[:, half, at, kind]
                for kind in range(3)
                for half in range(2)
                for part, n in zip(pair_rows, each)
                for at in range(n)
            ],
            axis=1,
        ).astype(F32)
        grads = [g.reshape(2, -1, D) for g in (grad_out_a, grad_out_b)]
        grads = jnp.concatenate(grads, axis=1).reshape(count, 2, rows // 2, D).swapaxes(0, 1)
        sum_out = Chain(sum_steps(grads)).finish().reshape(rows, D).astype(F32)
    return (
        result, tokens_grad, vectors[0], vectors[1], sum_mix, mix_vector, sum_out, vectors[4],
        vectors[2], vectors[3], sum_rise, rise_vector, sum_fall, vectors[4],
    )


def solution(mesh):
    reps, count = mesh.devices.shape
    fine = Mesh(mesh.devices.reshape(reps // 4, 2, 2, count), (*REP, "shard"))
    rows = P((*REP, "shard"), None)
    line = P("shard")
    wide = P("shard", None)
    in_specs = (
        rows, rows, line, line, wide, line, wide, line, line, line, wide, line, wide, line, rows,
    )
    out_specs = (
        rows, rows, line, line, wide, line, wide, line, line, line, wide, line, wide, line,
    )
    return jax.shard_map(shards, mesh=fine, in_specs=in_specs, out_specs=out_specs, check_vma=False)
```

```python
import math

import jax
import jax.numpy as jnp
from jax import lax
from jax.experimental import pallas as pl
from jax.experimental.pallas import tpu as pltpu
from jax.sharding import Mesh
from jax.sharding import PartitionSpec as P

D = 768
HEADS = 12
HEAD_DIM = 64
ROT = 16
BLK = 256
PAIR = 2 * HEAD_DIM
PAIRS = HEADS // 2
SPAN = 3
EPS = 1e-05
F32 = jnp.float32
BF16 = jnp.bfloat16
REP = ("z", "x", "c")
VMEM_LIMIT = 56 * 1024 * 1024


def dot_nt(left, right):
    return lax.dot_general(left, right, (((1,), (1,)), ((), ())), preferred_element_type=F32)


def dot_nn(left, right):
    return lax.dot_general(left, right, (((1,), (0,)), ((), ())), preferred_element_type=F32)


def dot_tn(left, right):
    return lax.dot_general(left, right, (((0,), (0,)), ((), ())), preferred_element_type=F32)


def mlp_kernel(
    low_ref, low_t_ref, cot_ref, rise_ref, bias_ref, fall_ref, *rest, per_shard, count,
):
    act_ref, back_ref, grads_ref, total_ref, slope = rest[-5:]
    at = pl.program_id(0)
    tile = rise_ref.shape[1]
    before = dot_nn(low_ref[...], rise_ref[...]) + bias_ref[...]
    chance = 0.5 + 0.5 * lax.erf(before * (1.0 / math.sqrt(2.0)))
    slope[...] = chance + before * jnp.exp(-0.5 * before * before) * (1.0 / math.sqrt(2.0 * math.pi))
    act_ref[...] = (before * chance).astype(BF16)
    grad_fall = dot_tn(act_ref[...], cot_ref[...]).astype(BF16)
    owner_fall = at // per_shard
    place = pl.ds(pl.multiple_of(lax.rem(at, per_shard) * tile, tile), tile)
    grads_ref[owner_fall, 0, place, :] = grad_fall
    back_ref[...] = (dot_nt(cot_ref[...], fall_ref[...]) * slope[...]).astype(BF16)
    low_grad = back_ref[...]
    total_ref[...] = jnp.sum(low_grad.astype(F32), axis=0, keepdims=True)
    grad_rise = dot_nn(low_t_ref[...], low_grad).astype(BF16)
    rows = D // count
    wide = D // tile
    block = at // wide
    cols = pl.ds(pl.multiple_of(lax.rem(at, wide) * tile, tile), tile)
    for owner in range(count):
        at_rows = pl.ds(pl.multiple_of(block * rows, rows), rows)
        grads_ref[owner, 1, at_rows, cols] = grad_rise[owner * rows : (owner + 1) * rows, :]


def mlp(low, low_t, cot, rise, bias, fall, waits):
    length = low.shape[0]
    hidden = rise.shape[1]
    count = lax.axis_size("shard")
    width = hidden // count
    tile = 256 if width % 256 == 0 else 128
    whole = pl.BlockSpec((length, D), lambda at: (0, 0))
    column = pl.BlockSpec((length, tile), lambda at: (0, at))
    line = pl.BlockSpec((1, tile), lambda at: (0, at))
    return pl.pallas_call(
        lambda *refs: mlp_kernel(*refs, per_shard=width // tile, count=count),
        grid=(hidden // tile,),
        in_specs=[
            whole,
            pl.BlockSpec((D, length), lambda at: (0, 0)),
            whole,
            pl.BlockSpec((D, tile), lambda at: (0, at)),
            line,
            pl.BlockSpec((tile, D), lambda at: (at, 0)),
        ]
        + [pl.BlockSpec(memory_space=pl.ANY)] * len(waits),
        out_specs=[
            column,
            column,
            pl.BlockSpec((count, 2, width, D), lambda at: (0, 0, 0, 0)),
            line,
        ],
        out_shape=[
            jax.ShapeDtypeStruct((length, hidden), BF16),
            jax.ShapeDtypeStruct((length, hidden), BF16),
            jax.ShapeDtypeStruct((count, 2, width, D), BF16),
            jax.ShapeDtypeStruct((1, hidden), F32),
        ],
        scratch_shapes=[pltpu.VMEM((length, tile), F32)],
        compiler_params=pltpu.CompilerParams(vmem_limit_bytes=VMEM_LIMIT),
        cost_estimate=pl.CostEstimate(
            flops=8 * length * D * hidden,
            bytes_accessed=6 * length * D + 8 * D * hidden + 4 * length * hidden,
            transcendentals=2 * length * hidden,
        ),
        name="mlp",
    )(low, low_t, cot, rise, bias, fall, *waits)


def attention_kernel(
    first_ref, low_ref, low_t_ref, cot_ref, wq_ref, wk_ref, wv_ref, bq_ref, bk_ref, bv_ref, out_w_ref,
    cos_ref, up_ref, down_ref, start_ref, *rest, each, count,
):
    (
        ob, back, grads_ref, grad_out_ref, total_ref, qs, ks, vs, kt, vt, dk, dv, gs, ot, w3,
    ) = rest[-15:]
    length = low_ref.shape[0]
    half = ROT // 2
    scale = HEAD_DIM ** -0.5

    def turn(x):
        return (
            x * cos_ref[...]
            + pltpu.roll(x, PAIR - half, 1) * up_ref[...]
            + pltpu.roll(x, half, 1) * down_ref[...]
        )

    def turn_back(g, rows):
        return (
            g * cos_ref[rows, :]
            + pltpu.roll(g * up_ref[rows, :], half, 1)
            + pltpu.roll(g * down_ref[rows, :], PAIR - half, 1)
        )

    w3[:, :PAIR] = wq_ref[...]
    w3[:, PAIR : 2 * PAIR] = wk_ref[...]
    w3[:, 2 * PAIR :] = wv_ref[...]
    mixed = dot_nn(low_ref[...], w3[...])
    qs[...] = turn(mixed[:, :PAIR] + bq_ref[...]).astype(BF16)
    keys = turn(mixed[:, PAIR : 2 * PAIR] + bk_ref[...]).astype(BF16)
    ks[...] = keys
    kt[...] = keys.astype(F32).T.astype(BF16)
    values = (mixed[:, 2 * PAIR :] + bv_ref[...]).astype(BF16)
    vs[...] = values
    vt[...] = values.astype(F32).T.astype(BF16)
    gs[...] = dot_nt(cot_ref[...], out_w_ref[...]).astype(BF16)
    dk[...] = jnp.zeros_like(dk)
    dv[...] = jnp.zeros_like(dv)
    low = lax.broadcasted_iota(jnp.int32, (BLK, PAIR), 1) < HEAD_DIM

    def block(at, blocks):
        extent = blocks * BLK
        query_at = pl.multiple_of(at * BLK, BLK)
        key_at = pl.multiple_of((at - blocks + 1) * BLK, BLK)
        rows = pl.ds(query_at, BLK)
        cols = pl.ds(key_at, extent)
        qb = qs[rows, :]
        gb = gs[rows, :]
        kb = ks[cols, :]
        vb = vs[cols, :]
        start = start_ref[:, rows]
        key_index = lax.broadcasted_iota(jnp.int32, (extent, BLK), 0)
        query_index = lax.broadcasted_iota(jnp.int32, (extent, BLK), 1) + (blocks - 1) * BLK
        allowed = (key_index >= start - key_at) & (key_index <= query_index)
        outs, dqs = [], []
        dk_new = dv_new = None
        for head in range(2):
            lanes = low if head == 0 else ~low
            part = slice(head * HEAD_DIM, (head + 1) * HEAD_DIM)
            qh = jnp.where(lanes, qb, jnp.zeros_like(qb))
            gh = jnp.where(lanes, gb, jnp.zeros_like(gb))
            scores = jnp.where(allowed, dot_nt(kb, qh) * (scale * math.log2(math.e)), -1e30)
            weight = jnp.exp2(scores - jnp.max(scores, axis=0, keepdims=True))
            probs = weight * (1.0 / jnp.sum(weight, axis=0, keepdims=True))
            low_probs = probs.astype(BF16)
            outs.append(dot_nn(vt[part, cols], low_probs))
            grad_probs = dot_nt(vb, gh)
            delta = jnp.sum(probs * grad_probs, axis=0, keepdims=True)
            grad_scores = (probs * (grad_probs - delta)).astype(BF16)
            dqs.append(dot_nn(kt[part, cols], grad_scores))
            dv_part = dot_nn(low_probs, gh)
            dk_part = dot_nn(grad_scores, qh)
            dv_new = dv_part if dv_new is None else dv_new + dv_part
            dk_new = dk_part if dk_new is None else dk_new + dk_part
        dv[cols, :] += dv_new
        dk[cols, :] += dk_new
        out_t = jnp.concatenate(outs, 0)
        ot[:, rows] = out_t.astype(BF16)
        ob[rows, :] = out_t.T.astype(BF16)
        back[0, rows, :] = turn_back(jnp.concatenate(dqs, 0).T * scale, rows).astype(BF16)

    def step(at, carry):
        needed = at - first_ref[at] + 1
        for blocks in range(1, SPAN + 1):
            pl.when(needed == blocks)(lambda blocks=blocks: block(at, blocks))
        return carry

    lax.fori_loop(0, length // BLK, step, 0)
    back[1] = turn_back(dk[...] * scale, slice(None)).astype(BF16)
    back[2] = dv[...].astype(BF16)
    grad_mixed = jnp.concatenate([back[0], back[1], back[2]], axis=1)
    total_ref[...] = jnp.sum(grad_mixed.astype(F32), axis=0, keepdims=True)
    grad_w = dot_nn(low_t_ref[...], grad_mixed).astype(BF16)
    grad_out = dot_nn(ot[...], cot_ref[...]).astype(BF16)
    grad_out_ref[...] = grad_out
    at = pl.program_id(0)
    rows = D // count
    split = grads_ref.shape[2]
    cols = pl.ds(pl.multiple_of(at * 3 * PAIR, PAIR), 3 * PAIR)
    for owner in range(count):
        own = grad_w[owner * rows : (owner + 1) * rows, :]
        grads_ref[0, owner, :, cols] = own[:split]
        grads_ref[1, owner, : rows - split, cols] = own[split:]
    if 2 * split > rows:
        cols = pl.ds(pl.multiple_of(lax.rem(at, each) * D, D), D)
        grads_ref[1, at // each, rows - split :, cols] = grad_out


def attention(low, low_t, cot, both, mix_bias, tables, start, first, each, shared, waits):
    length = low.shape[0]
    count = lax.axis_size("shard")
    first_block = start[0, ::BLK] // BLK
    rows = D // count
    joint = count == 2

    def pair(at):
        return at // each * (PAIRS // 2) + first + at % each

    def weight(offset):
        return pl.BlockSpec((D, PAIR), lambda at, _: (0, offset + pair(at)))

    def bias(offset):
        return pl.BlockSpec((1, PAIR), lambda at, _: (0, offset + pair(at)))

    def fixed(*shape):
        return pl.BlockSpec(shape, lambda at, _: (0,) * len(shape))

    pairs = 2 * each
    grads = (2, count, (rows + (PAIR if joint else 0)) // 2, pairs * 3 * PAIR)
    return pl.pallas_call(
        lambda *refs: attention_kernel(*refs, each=each, count=count),
        grid_spec=pltpu.PrefetchScalarGridSpec(
            num_scalar_prefetch=1,
            grid=(pairs,),
            in_specs=[
                fixed(length, D), fixed(D, length), fixed(length, D),
                weight(0), weight(PAIRS), weight(2 * PAIRS),
                bias(0), bias(PAIRS), bias(2 * PAIRS),
                pl.BlockSpec((PAIR, D), lambda at, _: (pair(at), 3)),
                fixed(length, PAIR), fixed(length, PAIR), fixed(length, PAIR), fixed(1, length),
            ]
            + [pl.BlockSpec(memory_space=pl.ANY)] * len((*shared, *waits)),
            out_specs=[
                pl.BlockSpec((length, PAIR), lambda at, _: (0, pair(at))),
                pl.BlockSpec((3, length, PAIR), lambda at, _: (0, 0, pair(at))),
                fixed(*grads),
                pl.BlockSpec((PAIR, D), lambda at, _: (at, 0)),
                pl.BlockSpec((1, 3 * PAIR), lambda at, _: (0, pair(at))),
            ],
            scratch_shapes=[pltpu.VMEM((length, PAIR), BF16)] * 3
            + [pltpu.VMEM((PAIR, length), BF16)] * 2
            + [pltpu.VMEM((length, PAIR), F32)] * 2
            + [
                pltpu.VMEM((length, PAIR), BF16), pltpu.VMEM((PAIR, length), BF16),
                pltpu.VMEM((D, 3 * PAIR), BF16),
            ],
        ),
        out_shape=[
            jax.ShapeDtypeStruct((length, D), BF16),
            jax.ShapeDtypeStruct((3, length, D), BF16),
            jax.ShapeDtypeStruct(grads, BF16),
            jax.ShapeDtypeStruct((pairs * PAIR, D), BF16),
            jax.ShapeDtypeStruct((1, 3 * D), F32),
        ],
        compiler_params=pltpu.CompilerParams(vmem_limit_bytes=VMEM_LIMIT),
        cost_estimate=pl.CostEstimate(
            flops=pairs * (20 * length * D * PAIR + 12 * length * 640 * HEAD_DIM * 16),
            bytes_accessed=6 * length * D + pairs * (D * PAIR * 16 + length * PAIR * 8),
            transcendentals=pairs * 2 * length * 640,
        ),
        input_output_aliases=dict(zip((15, 16, 17), (0, 1, 4))) if shared else {},
        name="attention",
    )(
        first_block, low, low_t, cot, both, both, both, mix_bias, mix_bias, mix_bias, both, *tables,
        start, *shared, *waits,
    )


def errors_kernel(
    grad_ref, rise_ref, back_ref, both_ref, tokens_ref, cot_ref, gain_one_ref, gain_two_ref, *rest,
):
    out_ref, sums_ref = rest[-2:]
    inputs = tokens_ref[...].astype(F32)
    upstream = cot_ref[...].astype(F32)
    center = inputs - jnp.mean(inputs, axis=-1, keepdims=True)
    inverse = lax.rsqrt(jnp.mean(center * center, axis=-1, keepdims=True) + EPS)
    unit = center * inverse
    error_two = dot_nt(grad_ref[...], rise_ref[...])
    error_one = dot_nt(back_ref[0], both_ref[:, :D])
    error_one += dot_nt(back_ref[1], both_ref[:, D : 2 * D])
    error_one += dot_nt(back_ref[2], both_ref[:, 2 * D :])
    total = upstream
    for error, gain_ref in ((error_one, gain_one_ref), (error_two, gain_two_ref)):
        scaled = error * gain_ref[...]
        total += inverse * (
            scaled
            - jnp.mean(scaled, axis=-1, keepdims=True)
            - unit * jnp.mean(scaled * unit, axis=-1, keepdims=True)
        )
    out_ref[...] = total
    sums = [error_one * unit, error_one, error_two * unit, error_two, upstream]

    @pl.when(pl.program_id(0) == 0)
    def _():
        sums_ref[...] = jnp.zeros_like(sums_ref)

    for row, value in enumerate(sums):
        sums_ref[row : row + 1, :] += jnp.sum(value, axis=0, keepdims=True)


def input_errors(grad, rise, back, both, tokens, cot, gain_one, gain_two, waits):
    length, hidden = grad.shape

    def rows(wide):
        return pl.BlockSpec((BLK, wide), lambda at: (at, 0))

    def fixed(*shape):
        return pl.BlockSpec(shape, lambda at: (0,) * len(shape))

    return pl.pallas_call(
        errors_kernel,
        grid=(length // BLK,),
        in_specs=[
            rows(hidden), fixed(D, hidden), pl.BlockSpec((3, BLK, D), lambda at: (0, at, 0)),
            fixed(D, 3 * D), rows(D), rows(D), fixed(1, D), fixed(1, D),
        ]
        + [pl.BlockSpec(memory_space=pl.ANY)] * len(waits),
        out_specs=[rows(D), fixed(8, D)],
        out_shape=[jax.ShapeDtypeStruct((length, D), F32), jax.ShapeDtypeStruct((8, D), F32)],
        compiler_params=pltpu.CompilerParams(vmem_limit_bytes=VMEM_LIMIT),
        cost_estimate=pl.CostEstimate(flops=1000, bytes_accessed=1000, transcendentals=0),
        name="input_errors",
    )(grad, rise, back, both, tokens, cot, gain_one, gain_two, *waits)


def output_kernel(act_ref, fall_ref, heads_ref, out_w_ref, tokens_ref, bias_ref, *rest):
    branches = dot_nn(act_ref[...], fall_ref[...]) + dot_nn(heads_ref[...], out_w_ref[...])
    total = tokens_ref[...].astype(F32) + branches + bias_ref[...]
    rest[-2][...] = total.astype(BF16)
    rest[-1][...] = total[:1, :PAIR]


def block_output(act, fall, heads, both, tokens, bias, waits):
    length, hidden = act.shape

    def rows(wide):
        return pl.BlockSpec((BLK, wide), lambda at: (at, 0))

    return pl.pallas_call(
        output_kernel,
        grid=(length // BLK,),
        in_specs=[
            rows(hidden), pl.BlockSpec((hidden, D), lambda at: (0, 0)), rows(D),
            pl.BlockSpec((D, D), lambda at: (0, 3)), rows(D), pl.BlockSpec((1, D), lambda at: (0, 0)),
        ]
        + [pl.BlockSpec(memory_space=pl.ANY)] * len(waits),
        out_specs=[rows(D), pl.BlockSpec((1, PAIR), lambda at: (0, 0))],
        out_shape=[
            jax.ShapeDtypeStruct((length, D), BF16), jax.ShapeDtypeStruct((1, PAIR), F32),
        ],
        compiler_params=pltpu.CompilerParams(vmem_limit_bytes=VMEM_LIMIT),
        cost_estimate=pl.CostEstimate(flops=1000, bytes_accessed=1000, transcendentals=0),
        name="block_output",
    )(act, fall, heads, both, tokens, bias, *waits)


def widen_mlp_kernel(fall_ref, rise_ref, fall_out, rise_out, mark_ref):
    fall_out[...] = fall_ref[0].astype(F32)
    rise_out[...] = rise_ref[0].astype(F32)
    mark_ref[...] = fall_out[:1, :PAIR]


def widen_mlp(owned):
    _, width, _ = owned.shape
    rows = D // lax.axis_size("shard")
    return pl.pallas_call(
        widen_mlp_kernel,
        grid=(width // rows,),
        in_specs=[pl.BlockSpec((1, rows, D), lambda at, kind=kind: (kind, at, 0)) for kind in (0, 1)],
        out_specs=[
            pl.BlockSpec((rows, D), lambda at: (at, 0)),
            pl.BlockSpec((rows, D), lambda at: (0, at)),
            pl.BlockSpec((1, PAIR), lambda at: (0, 0)),
        ],
        out_shape=[
            jax.ShapeDtypeStruct((width, D), F32),
            jax.ShapeDtypeStruct((rows, width // rows * D), F32),
            jax.ShapeDtypeStruct((1, PAIR), F32),
        ],
        name="widen_mlp",
    )(owned, owned)


def widen_mix_kernel(first_ref, second_ref, mix_out, out_out):
    rows = mix_out.shape[0]
    third = PAIRS // 2
    for pair in range(PAIRS):
        half, at = pair // third, pair % third
        ref, place = (first_ref, half * 2 + at) if at < 2 else (second_ref, half)
        for kind in range(3):
            to = (kind * PAIRS + pair) * PAIR
            source = (place * 3 + kind) * PAIR
            mix_out[:, to : to + PAIR] = ref[:rows, source : source + PAIR].astype(F32)
    for at in range(third):
        ref, source = (first_ref, at * D) if at < 2 else (second_ref, 0)
        out_out[at * PAIR : (at + 1) * PAIR, :] = ref[rows:, source : source + D].astype(F32)


def widen_mix(first, second):
    rows = D // lax.axis_size("shard")
    return pl.pallas_call(
        widen_mix_kernel,
        out_shape=[jax.ShapeDtypeStruct((rows, 3 * D), F32), jax.ShapeDtypeStruct((rows, D), F32)],
        compiler_params=pltpu.CompilerParams(vmem_limit_bytes=VMEM_LIMIT),
        name="widen_mix",
    )(first, second)


def rotary_tables(segments):
    length = segments.shape[1]
    half = ROT // 2
    position = jnp.arange(length, dtype=jnp.int32)[None]
    change = jnp.concatenate(
        [jnp.ones((1, 1), dtype=bool), segments[:, 1:] != segments[:, :-1]], axis=1
    )
    start = lax.cummax(jnp.where(change, position, 0), axis=1)
    place = (position - start).astype(F32)
    frequency = 10000.0 ** (-2.0 * jnp.arange(half, dtype=F32) / ROT)
    angles = place[0][:, None] * frequency
    cosine, sine = jnp.cos(angles), jnp.sin(angles)
    rest = HEAD_DIM - ROT
    zero = jnp.zeros((length, half), F32)
    zeros = jnp.zeros((length, rest), F32)
    tables = (
        jnp.concatenate([cosine, cosine, jnp.ones((length, rest), F32)], axis=1),
        jnp.concatenate([-sine, zero, zeros], axis=1),
        jnp.concatenate([zero, sine, zeros], axis=1),
    )
    return start, [jnp.tile(table, (1, 2)) for table in tables]


def tie(value, *others):
    return lax.optimization_barrier((value, *others))[0]


def bit_of(axis, mask):
    return (lax.axis_index(axis) // mask) % 2


def swap(value, axis, mask):
    size = lax.axis_size(axis)
    return lax.ppermute(value, axis, [(i, i ^ mask) for i in range(size)])


def log2(size):
    return size.bit_length() - 1


class Chain:
    def __init__(self, steps):
        self.steps = steps
        self.result = None
        self.last = None

    def step(self, *after):
        if self.result is not None:
            return self.last
        try:
            self.last = next(self.steps) if self.last is None else self.steps.send(after)
        except StopIteration as stop:
            self.result = self.last = stop.value
        return self.last

    def finish(self, *after):
        while self.result is None:
            self.step(*after)
        return self.result


def arrived(value, after):
    return tie(value, *after) if after else value


def joined(mine, other, bit):
    return jnp.where(bit == 1, jnp.stack([other, mine]), jnp.stack([mine, other]))


def own_part(weight):
    parts = lax.axis_size("x") * lax.axis_size("c")
    rows = weight.shape[0] // parts
    at = lax.axis_index(("x", "c")) * rows
    return lax.dynamic_slice_in_dim(weight, at, rows, axis=0)


def gather_rows(weight):
    return lax.all_gather(own_part(weight), ("shard", "x", "c"), axis=0, tiled=True)


def gather_steps(weight, *after):
    other = own_part(weight)
    other = tie(other, *after) if after else other
    got = swap(other, "shard", 1)
    other = arrived(got, (yield other))
    for axis, at in (("x", 0), ("c", 1)):
        got = swap(other, axis, 1)
        got = arrived(got, (yield other))
        bit = lax.axis_index(axis)
        other = jnp.where(
            bit == 1, jnp.stack([got, other], at), jnp.stack([other, got], at)
        )
    other = other.reshape(weight.shape)
    return joined(weight, other, lax.axis_index("shard")).reshape(-1, weight.shape[1])


def sum_steps(grads, late=()):
    dims = [("c", 1)]
    dims += [("shard", 1 << i) for i in reversed(range(log2(lax.axis_size("shard"))))]
    rep = [("x", 1)] + [("z", 1 << i) for i in range(log2(lax.axis_size("z")))]
    parts = grads
    for dim in dims + rep:
        half = parts.reshape(2, -1, grads.shape[-1])
        bit = bit_of(*dim)
        send = lax.dynamic_index_in_dim(half, 1 - bit, axis=0, keepdims=False)
        got = swap(send, *dim)
        got = arrived(got, (yield send))
        keep = lax.dynamic_index_in_dim(half, bit, axis=0, keepdims=False)
        parts = (keep.astype(F32) + got.astype(F32)).astype(BF16)
    for dim in rep[::-1] + dims[:1]:
        got = swap(parts, *dim)
        after = yield parts
        got = arrived(got, (*after, *(late if dim == rep[0] else ())))
        parts = joined(parts, got, bit_of(*dim)).reshape(-1, grads.shape[-1])
    return parts.reshape(2, -1, grads.shape[-1])


def sum_offloaded(grads):
    parts = grads.reshape(-1, grads.shape[-1])
    parts = lax.psum_scatter(parts, ("shard", "c", "x"), scatter_dimension=0, tiled=True)
    yield parts
    parts = lax.psum_scatter(parts, "z", scatter_dimension=0, tiled=True)
    parts = arrived(parts, (yield parts))
    yield parts
    parts = lax.all_gather(parts, ("c", "x", "z"), axis=0, tiled=True)
    return parts.reshape(grads.shape[1:])


def total_steps(totals):
    rep = [("c", 1), ("x", 1)] + [("z", 1 << i) for i in range(log2(lax.axis_size("z")))]
    parts = totals
    for mask in [1 << i for i in reversed(range(log2(totals.shape[0])))]:
        half = parts.reshape(2, -1)
        bit = bit_of("shard", mask)
        send = lax.dynamic_index_in_dim(half, 1 - bit, axis=0, keepdims=False).astype(BF16)
        got = swap(send, "shard", mask)
        got = arrived(got, (yield send))
        parts = lax.dynamic_index_in_dim(half, bit, axis=0, keepdims=False) + got.astype(F32)
    for dim in rep:
        sent = parts.reshape(-1).astype(BF16)
        got = swap(sent, *dim)
        got = arrived(got, (yield sent))
        parts = sent.astype(F32) + got.astype(F32)
    return parts


def shards(
    tokens, segments, attn_gain, attn_shift, qkv_weight, qkv_bias, proj_weight, proj_bias,
    mlp_gain, mlp_shift, up_weight, up_bias, down_weight, down_bias, cotangent,
):
    count = lax.axis_size("shard")
    joint = count == 2
    small = [attn_gain, attn_shift, qkv_bias, proj_bias, mlp_gain, mlp_shift, up_bias, down_bias]
    sizes = [vector.shape[0] for vector in small]
    edges = [sum(sizes[:i]) for i in range(len(sizes) + 1)]
    own_small = jnp.concatenate(small)[None]
    own_both = jnp.concatenate([qkv_weight, proj_weight], axis=1)
    if joint:
        small_all = joined(own_small, swap(own_small, "shard", 1), lax.axis_index("shard"))
        small_all = small_all.reshape(2, -1)
        rise_chain, fall_chain, both_chain = [
            Chain(gather_steps(weight)) for weight in (up_weight, down_weight, own_both)
        ]
        rise_chain.step()
        mark = rise_chain.step()
        fall_chain.steps = gather_steps(down_weight, mark)
        fall_chain.step()
        rise_chain.step()
        mark = fall_chain.step()
        both_chain.steps = gather_steps(own_both, mark)
        both_chain.step()
        rise = rise_chain.finish()
        mark = fall_chain.step()
        both_chain.step(mark)
        fall = fall_chain.finish()
    else:
        small_all = lax.all_gather(own_small, "shard", axis=0, tiled=True)
        rise, fall, both = [gather_rows(w) for w in (up_weight, down_weight, own_both)]
    gain_one, shift_one, mix_bias, out_bias, gain_two, shift_two, rise_bias, fall_bias = [
        small_all[:, a:b].reshape(1, -1).astype(F32) for a, b in zip(edges[:-1], edges[1:])
    ]

    inputs = tokens.astype(F32)
    start, tables = rotary_tables(segments)
    center = inputs - jnp.mean(inputs, axis=-1, keepdims=True)
    inverse = lax.rsqrt(jnp.mean(center * center, axis=-1, keepdims=True) + EPS)
    unit = center * inverse
    low_one = (unit * gain_one + shift_one).astype(BF16)
    low_two = (unit * gain_two + shift_two).astype(BF16)
    low_one_t = low_one.T
    low_two_t = low_two.T
    rows = D // count
    each = (2, 1)
    waits = (both_chain.last,) if joint else ()
    act, act_back, mlp_grads, rise_total = mlp(
        low_two, low_two_t, cotangent, rise, rise_bias, fall, waits
    )
    mlp_chain = Chain(sum_offloaded(mlp_grads))
    scattered = mlp_chain.step()
    if joint:
        both_chain.step(rise_total)
        both = both_chain.finish()

    def attend(first, each, shared, *waits):
        return attention(
            low_one, low_one_t, cotangent, both, mix_bias, tables, start, first, each, shared, waits
        )

    out_a, back_a, grads_a, grad_out_a, total_a = attend(0, each[0], (), rise_total)
    late = []
    sum_a = Chain(sum_steps(grads_a, late))
    sum_a.step()
    sent = sum_a.step()
    heads, back, grads_b, grad_out_b, mix_total = attend(
        each[0], each[1], (out_a, back_a, total_a), sent, scattered
    )
    sum_b = Chain(sum_steps(grads_b, late))
    sum_b.step()
    mlp_chain.step()
    marks = [mlp_chain.step(mix_total), sum_a.step(mix_total), sum_b.step()]
    tokens_grad, sums = input_errors(
        act_back, rise, back, both, tokens, cotangent, gain_one, gain_two, marks
    )
    mlp_own = mlp_chain.finish()
    sum_fall, sum_rise, widened = widen_mlp(mlp_own)
    late.append(widened)
    mix_total = mix_total.reshape(PAIRS, 3, PAIR).swapaxes(0, 1)
    totals = [sums[:5].reshape(5, count, rows).swapaxes(0, 1), mix_total, rise_total]
    totals = jnp.concatenate([t.reshape(count, -1) for t in totals], axis=1)
    total_chain = Chain(total_steps(totals))
    marks = [total_chain.step(), sum_b.step(sums), sum_a.step(sums)]
    result, mark = block_output(act, fall, heads, both, tokens, out_bias + fall_bias, marks)
    for chain in (total_chain, sum_b, sum_a):
        chain.step(mark)
    owned = total_chain.finish()
    mix_own = [sum_a.finish(), sum_b.finish()]
    vectors = owned[: 5 * rows].reshape(5, rows)
    mix_vector, rise_vector = owned[5 * rows : 8 * rows], owned[8 * rows :]

    mix_own = [own.reshape(-1, own.shape[-1]) for own in mix_own]
    if joint:
        sum_mix, sum_out = widen_mix(*mix_own)
    else:
        pair_rows = [own[:rows].reshape(rows, 2, n, 3, PAIR) for own, n in zip(mix_own, each)]
        sum_mix = jnp.concatenate(
            [
                part[:, half, at, kind]
                for kind in range(3)
                for half in range(2)
                for part, n in zip(pair_rows, each)
                for at in range(n)
            ],
            axis=1,
        ).astype(F32)
        grads = [g.reshape(2, -1, D) for g in (grad_out_a, grad_out_b)]
        grads = jnp.concatenate(grads, axis=1).reshape(count, 2, rows // 2, D).swapaxes(0, 1)
        sum_out = Chain(sum_steps(grads)).finish().reshape(rows, D).astype(F32)
    return (
        result, tokens_grad, vectors[0], vectors[1], sum_mix, mix_vector, sum_out, vectors[4],
        vectors[2], vectors[3], sum_rise, rise_vector, sum_fall, vectors[4],
    )


def solution(mesh):
    reps, count = mesh.devices.shape
    fine = Mesh(mesh.devices.reshape(reps // 4, 2, 2, count), (*REP, "shard"))
    rows = P((*REP, "shard"), None)
    line = P("shard")
    wide = P("shard", None)
    in_specs = (
        rows, rows, line, line, wide, line, wide, line, line, line, wide, line, wide, line, rows,
    )
    out_specs = (
        rows, rows, line, line, wide, line, wide, line, line, line, wide, line, wide, line,
    )
    return jax.shard_map(shards, mesh=fine, in_specs=in_specs, out_specs=out_specs, check_vma=False)
```
